128 devices in a mesh: pts: 8 (over z, x_hi), lmk: 16 (over y, x_lo, core).
Axes of the slice: x: 4 (x_hi: 2, x_lo: 2; x = x_hi * 2 + x_lo), y: 4, z: 4, core: 2. Of those that a mesh axis runs over, the one named last changes fastest.
Arguments:
- points: bfloat16 [262144, 128], P('pts'), may hold values from -3.5 to 3.5
- landmark_ids: int32 [16384], P('lmk'), may hold values from 0 to 262143, as said below
- coefficients: bfloat16 [16384, 32], P('lmk'), may hold values from -192 to 192
Outputs:
- product: float32 [16384, 32], P(('lmk', 'pts'))
The draws below stay inside these ranges and needn't reach their ends.
Inputs may be any that keep to these rules, and one draw needn't show every extreme that they name: `landmark_ids`: landmarks fall unevenly on the point blocks of 32768 rows; indices may repeat; 0 and 262143 occur in every draw.
All inputs are finite; a program needn't handle non-finite values.
Results may differ from the reference program's by a relative error of at most 0.00045.
Values may be sent and summed in bfloat16 or wider, within the bound.
A program may use at most 128 MiB of HBM per device.

```python
import jax
import jax.numpy as jnp
from jax import lax

D = 128
OUTS = 32
PTS_DEV = 32768
BLOCK = 2048
M = 16384
NPTS = 262144


def draw_points(key, part):
    key = jax.random.fold_in(key, 5)
    key_cols, key_vals = jax.random.split(key, 2)
    column_rank = jax.random.permutation(key_cols, D)
    latent = (column_rank < D // 8)[None, :]
    sample = jax.random.normal(key_vals, (NPTS, D), jnp.float32)
    values = jnp.where(latent, sample * 0.775, sample * 0.168)
    return jnp.clip(values, -3.5, 3.5).astype(jnp.bfloat16)


def draw_landmark_ids(key, part):
    key = jax.random.fold_in(key, 11)
    k_order, k_pick, k_offset, k_spot = jax.random.split(key, 4)
    owners = NPTS // PTS_DEV
    order = jax.random.permutation(k_order, owners)
    weight = 1 + 3 * order
    limits = jnp.cumsum(weight)
    pick = jax.random.randint(k_pick, (M,), 0, limits[-1])
    owner = jnp.sum((pick[:, None] >= limits[None, :]).astype(jnp.int32), axis=1)
    offset = jax.random.randint(k_offset, (M,), 0, PTS_DEV)
    ids = (owner * PTS_DEV + offset).astype(jnp.int32)
    spot = jax.random.randint(k_spot, (), 0, M)
    ids = ids.at[spot].set(0)
    ids = ids.at[(spot + M // 2) % M].set(NPTS - 1)
    return ids


def block_levels(own_key, shape, pieces, low, top_value):
    loudness, own = 1.0, jax.random.fold_in(own_key, 6)
    for axis_at, shards_of in pieces:
        draws = jnp.exp(jax.random.uniform(jax.random.fold_in(own, axis_at), (shards_of,), jnp.float32, low / len(pieces), top_value / len(pieces)))
        loudness = loudness * jnp.repeat(draws, shape[axis_at] // shards_of).reshape([-1 if axis == axis_at else 1 for axis in range(len(shape))])
    return loudness


def centred(stream_key, extent, scale, bound, cuts=(), dtype=jnp.bfloat16):
    gain = block_levels(stream_key, extent, cuts, -0.22, 0.18) if cuts else 1.0
    drawn = jax.random.normal(stream_key, extent, jnp.float32) * scale * gain
    return jnp.minimum(jnp.maximum(drawn, -bound), bound).astype(dtype)


def setup_inputs(seed: int = 0) -> dict:
    splits = jax.random.split(jax.random.key(seed), 4)
    return {
        "points": draw_points(jax.random.fold_in(splits[3], 71), 0),
        "landmark_ids": draw_landmark_ids(jax.random.fold_in(splits[3], 71), 0),
        "coefficients": centred(splits[2], (M, OUTS), 32.0, 192.0, ((0, 16),)),
    }


GAMMA = 0.25


def kernel_tile(rows, centers, center_sq):
    cross = jnp.dot(rows, centers.T, preferred_element_type=jnp.float32)
    row_f = rows.astype(jnp.float32)
    row_sq = jnp.sum(row_f * row_f, axis=1)
    dist = row_sq[:, None] + center_sq[None, :] - 2.0 * cross
    return jnp.exp(-GAMMA * dist).astype(jnp.bfloat16)


def reference(points, landmark_ids, coefficients):
    centers = jnp.take(points, landmark_ids, axis=0)
    center_f = centers.astype(jnp.float32)
    center_sq = jnp.sum(center_f * center_f, axis=1)
    blocks = points.reshape(NPTS // BLOCK, BLOCK, D)

    def step(total, rows):
        tile = kernel_tile(rows, centers, center_sq)
        fitted = jnp.dot(tile, coefficients, preferred_element_type=jnp.float32).astype(jnp.bfloat16)
        part = lax.dot_general(tile, fitted, (((0,), (0,)), ((), ())), preferred_element_type=jnp.float32)
        return total + part, None

    total, unused = lax.scan(step, jnp.zeros((M, OUTS), jnp.float32), blocks)
    return total / NPTS
```

```python
import functools

import jax
import jax.numpy as jnp
from jax import lax
from jax.experimental import pallas as pl
from jax.experimental.pallas import tpu as pltpu
from jax.sharding import PartitionSpec as P

MESH = pl.DeviceIdType.MESH
BF16, F32 = jnp.bfloat16, jnp.float32
GROUPS = 8
CHUNK = 1024
STEP = 4096
PIECES = 2 * GROUPS
PIECE = STEP // PIECES
SLOTS = 4
NT = (((1,), (1,)), ((), ()))


def dot(a, b, dims=(((1,), (0,)), ((), ()))):
    return lax.dot_general(a, b, dims, preferred_element_type=F32)


def augment(rows_f):
    sq = -0.25 * jnp.sum(rows_f * rows_f, axis=1, keepdims=True)
    hi = sq.astype(BF16).astype(F32)
    mid = (sq - hi).astype(BF16).astype(F32)
    low = sq - hi - mid
    lane = lax.broadcasted_iota(jnp.int32, rows_f.shape, 1)
    return jnp.where(lane == 0, hi, jnp.where(lane == 1, mid, jnp.where(lane == 2, low, 0.0))).astype(BF16)


def square_row(rows):
    rows_f = rows.astype(F32)
    squares = rows_f * rows_f
    hi = squares.astype(BF16)
    low = (squares - hi.astype(F32)).astype(BF16)
    quarter = jnp.full((8, 2 * rows.shape[1]), -0.25, BF16)
    return dot(quarter, jnp.concatenate([hi, low], axis=1), NT)[:1]


def body(steps, picked, coef_t, points, out, xm, sq, ca, rows_in, centers, kt, part, p1r, p2s, p2r, fit, prod, prod_t,
         prod_in, load_sem, c_send, c_recv, s1, r1, s2, r2, s3, r3, s4, r4, o_send, o_recv):
    here = lax.axis_index("pts")
    lmk = lax.axis_index("lmk")
    chip, core = lmk // 2, lmk % 2
    other = chip * 2 + 1 - core

    def load(i):
        rows = pl.ds(i * STEP, STEP)
        return pltpu.make_async_copy(points.at[rows], xm.at[rows], load_sem.at[i])

    def start_load(i, carry):
        load(i).start()
        return carry

    lax.fori_loop(0, steps, start_load, 0)

    barrier = pltpu.get_barrier_semaphore()
    for k in range(GROUPS - 1):
        pl.semaphore_signal(barrier, inc=1, device_id={"pts": (here + k + 1) % GROUPS}, device_id_type=MESH)
        pl.semaphore_signal(barrier, inc=1, device_id={"lmk": ((chip + k + 1) % GROUPS) * 2 + core}, device_id_type=MESH)
    pl.semaphore_signal(barrier, inc=1, device_id={"lmk": other}, device_id_type=MESH)
    pl.semaphore_wait(barrier, 2 * GROUPS - 1)

    def along_pts(src, dst, send, recv, peer):
        return pltpu.make_async_remote_copy(src, dst, send, recv, device_id={"pts": peer}, device_id_type=MESH)

    def along_lmk(src, dst, send, recv, peer):
        return pltpu.make_async_remote_copy(src, dst, send, recv, device_id={"lmk": peer}, device_id_type=MESH)

    for k in range(GROUPS - 1):
        peer = (here + k + 1) % GROUPS
        along_pts(picked.at[peer], rows_in.at[k], c_send.at[0], c_recv.at[0], peer).start()

    def prepare(i, carry):
        load(i).wait()
        for h in range(STEP // CHUNK):
            rows = pl.ds(i * STEP + h * CHUNK, CHUNK)
            sq[i, :, pl.ds(h * CHUNK, CHUNK)] = square_row(xm[rows, :])
        return carry

    lax.fori_loop(0, steps // 2, prepare, 0)
    along_pts(rows_in, rows_in, c_send.at[0], c_recv.at[0], here).wait_recv()
    total = picked[here].astype(F32)
    for k in range(GROUPS - 1):
        total = total + rows_in[k].astype(F32)
    centers[here] = total.astype(BF16)
    for k in range(GROUPS - 1):
        peer = (here + k + 1) % GROUPS
        along_pts(centers.at[here], centers.at[here], c_send.at[1], c_recv.at[1], peer).start()
    lax.fori_loop(steps // 2, steps, prepare, 0)
    along_pts(rows_in, rows_in, c_send.at[1], c_recv.at[1], here).wait_recv()
    for g in range(GROUPS):
        rows_f = centers[g].astype(F32)
        ca[pl.ds(g * 128, 128), pl.ds(0, 128)] = (0.5 * rows_f).astype(BF16)
        ca[pl.ds(g * 128, 128), pl.ds(128, 128)] = augment(rows_f)
    prod[...] = jnp.zeros_like(prod)

    def copy1(b):
        return along_lmk(part.at[b, pl.ds((1 - core) * GROUPS, GROUPS)], p1r.at[b], s1.at[b], r1.at[b], other)

    def copy4(b):
        half = fit.at[b, pl.ds(core * GROUPS, GROUPS)]
        return along_lmk(half, half, s4.at[b], r4.at[b], other)

    def all2(b):
        return along_lmk(p2r.at[b], p2r.at[b], s2.at[b], r2.at[b], other)

    def all3(b):
        return along_lmk(p2r.at[b], p2r.at[b], s3.at[b], r3.at[b], other)

    lane = lax.broadcasted_iota(jnp.int32, (CHUNK, 128), 1)
    ones = jnp.where(lane < 3, 1.0, 0.0).astype(BF16)

    def step(t, carry):
        @pl.when(t >= SLOTS)
        def _():
            b = t - SLOTS
            copy4(b).wait_recv()
            fitted_t = jnp.concatenate([fit[b, q] for q in range(PIECES)], axis=1)
            prod[...] += dot(kt[b % SLOTS], fitted_t, NT)

        @pl.when(t < steps)
        def _():
            def tiles(h, carry):
                at = pl.multiple_of(t * STEP + h * CHUNK, CHUNK)
                rows = jnp.concatenate([xm[pl.ds(at, CHUNK), :], ones], axis=1)
                sq_row = sq[t, :, pl.ds(pl.multiple_of(h * CHUNK, CHUNK), CHUNK)]
                tile = jnp.exp(dot(ca[...], rows, NT) + sq_row).astype(BF16)
                kt[t % SLOTS, :, pl.ds(pl.multiple_of(h * CHUNK, CHUNK), CHUNK)] = tile
                partial_t = dot(coef_t[...], tile).astype(BF16)
                for q in range(CHUNK // PIECE):
                    part[t, h * (CHUNK // PIECE) + q] = partial_t[:, q * PIECE : (q + 1) * PIECE]
                return carry

            lax.fori_loop(0, STEP // CHUNK, tiles, 0)
            copy1(t).start()

        @pl.when((t >= 1) & (t < steps + 1))
        def _():
            b = t - 1
            copy1(b).wait_recv()
            for g in range(GROUPS):
                p2s[b, g] = (part[b, core * GROUPS + g].astype(F32) + p1r[b, g].astype(F32)).astype(BF16)
            for k in range(GROUPS - 1):
                peer = (chip + k + 1) % GROUPS
                along_lmk(p2s.at[b, peer], p2r.at[b, k], s2.at[b], r2.at[b], peer * 2 + core).start()

        @pl.when((t >= 2) & (t < steps + 2))
        def _():
            b = t - 2
            all2(b).wait_recv()
            total = p2s[b, chip].astype(F32)
            for k in range(GROUPS - 1):
                total = total + p2r[b, k].astype(F32)
            mine = core * GROUPS + chip
            fit[b, mine] = total.astype(BF16)
            for k in range(GROUPS - 1):
                peer = (chip + k + 1) % GROUPS
                along_lmk(fit.at[b, mine], fit.at[b, mine], s3.at[b], r3.at[b], peer * 2 + core).start()

        @pl.when((t >= 3) & (t < steps + 3))
        def _():
            b = t - 3
            all3(b).wait_recv()
            copy4(b).start()

        return carry

    lax.fori_loop(0, steps + SLOTS, step, 0)

    for g in range(GROUPS):
        prod_t[g] = prod[pl.ds(g * 128, 128), :].T
    for k in range(GROUPS - 1):
        peer = (here + k + 1) % GROUPS
        along_pts(prod_t.at[peer], prod_in.at[k], o_send, o_recv, peer).start()

    def sent(b, carry):
        copy1(b).wait_send()
        all2(b).wait_send()
        all3(b).wait_send()
        copy4(b).wait_send()
        return carry

    lax.fori_loop(0, steps, sent, 0)
    for i in range(2):
        along_pts(rows_in, rows_in, c_send.at[i], c_recv.at[i], here).wait_send()
    along_pts(prod_in, prod_in, o_send, o_recv, here).wait_recv()
    total = prod_t[here]
    for k in range(GROUPS - 1):
        total = total + prod_in[k]
    out[...] = total.T * (1.0 / (steps * STEP * GROUPS))
    along_pts(prod_in, prod_in, o_send, o_recv, here).wait_send()


def per_device(points, landmark_ids, coefficients):
    pts_rows, width = points.shape
    marks, outs_count = coefficients.shape
    steps = pts_rows // STEP
    here = lax.axis_index("pts")
    local_ids = landmark_ids - here * pts_rows
    owned = (local_ids >= 0) & (local_ids < pts_rows)
    picked = jnp.take(points, jnp.clip(local_ids, 0, pts_rows - 1), axis=0)
    picked = jnp.where(owned[:, None], picked, jnp.zeros((), BF16)).reshape(GROUPS, marks // GROUPS, width)
    vmem = pl.BlockSpec(memory_space=pltpu.VMEM)
    dma = pltpu.SemaphoreType.DMA
    return pl.pallas_call(
        functools.partial(body, steps),
        out_shape=jax.ShapeDtypeStruct((marks // GROUPS, outs_count), F32),
        in_specs=[vmem, vmem, pl.BlockSpec(memory_space=pl.ANY)],
        out_specs=vmem,
        scratch_shapes=[
            pltpu.VMEM((pts_rows, width), BF16),
            pltpu.VMEM((steps, 1, STEP), F32),
            pltpu.VMEM((marks, width + 128), BF16),
            pltpu.VMEM((GROUPS - 1, marks // GROUPS, width), BF16),
            pltpu.VMEM((GROUPS, marks // GROUPS, width), BF16),
            pltpu.VMEM((SLOTS, marks, STEP), BF16),
            pltpu.VMEM((steps, PIECES, outs_count, PIECE), BF16),
            pltpu.VMEM((steps, GROUPS, outs_count, PIECE), BF16),
            pltpu.VMEM((steps, GROUPS, outs_count, PIECE), BF16),
            pltpu.VMEM((steps, GROUPS - 1, outs_count, PIECE), BF16),
            pltpu.VMEM((steps, PIECES, outs_count, PIECE), BF16),
            pltpu.VMEM((marks, outs_count), F32),
            pltpu.VMEM((GROUPS, outs_count, 128), F32),
            pltpu.VMEM((GROUPS - 1, outs_count, 128), F32),
            dma((steps,)),
            dma((2,)),
            dma((2,)),
        ]
        + [dma((steps,))] * 8
        + [dma(()), dma(())],
        compiler_params=pltpu.CompilerParams(collective_id=0, has_side_effects=True, vmem_limit_bytes=60 * 2**20),
    )(picked, coefficients.T, points)


def solution(mesh):
    placed = (P("pts", None), P("lmk"), P("lmk", None))
    return jax.shard_map(
        per_device, mesh=mesh, in_specs=placed, out_specs=P(("lmk", "pts"), None), check_vma=False
    )
```

```python
import functools

import jax
import jax.numpy as jnp
from jax import lax
from jax.experimental import pallas as pl
from jax.experimental.pallas import tpu as pltpu
from jax.sharding import PartitionSpec as P

MESH = pl.DeviceIdType.MESH
BF16, F32 = jnp.bfloat16, jnp.float32
GROUPS = 8
TILE = 256
UNITS = 8
PIECES = 2 * UNITS
STEP = PIECES * TILE
SLOTS = 4
LAG = 3
SEG, RING = 128, 3
MXUS = (0, 1)


def augment(rows_f):
    sq = -0.25 * jnp.sum(rows_f * rows_f, axis=1, keepdims=True)
    hi = sq.astype(BF16).astype(F32)
    mid = (sq - hi).astype(BF16).astype(F32)
    low = sq - hi - mid
    lane = lax.broadcasted_iota(jnp.int32, rows_f.shape, 1)
    return jnp.where(lane == 0, hi, jnp.where(lane == 1, mid, jnp.where(lane == 2, low, 0.0))).astype(BF16)


def halves(rows):
    rows_f = rows.astype(F32)
    squares = rows_f * rows_f
    hi = squares.astype(BF16)
    return jnp.concatenate([hi, (squares - hi.astype(F32)).astype(BF16)], axis=1)


def body(steps, ids, coef, points, out, xm, sq, ca, ct, picked_f, picked, rows_in, centers, pb0, pb1, part, p1r, p2s, p2r,
         fit, prod_t, prod_in, load_sem, c_send, c_recv, s1, r1, s2, r2, s3, r3, s4, r4, o_send, o_recv):
    here = lax.axis_index("pts")
    lmk = lax.axis_index("lmk")
    chip, core = lmk // 2, lmk % 2
    other = chip * 2 + 1 - core
    slab, width = xm.shape
    marks = coef.shape[0]
    outs = coef.shape[1]
    pb = (pb0, pb1)

    def load(i):
        rows = pl.ds(i * STEP, STEP)
        return pltpu.make_async_copy(points.at[rows], xm.at[rows], load_sem.at[i])

    def start_load(i, carry):
        load(i).start()
        return carry

    lax.fori_loop(0, steps, start_load, 0)

    barrier = pltpu.get_barrier_semaphore()
    for k in range(GROUPS - 1):
        pl.semaphore_signal(barrier, inc=1, device_id={"pts": (here + k + 1) % GROUPS}, device_id_type=MESH)
        pl.semaphore_signal(barrier, inc=1, device_id={"lmk": ((chip + k + 1) % GROUPS) * 2 + core}, device_id_type=MESH)
    pl.semaphore_signal(barrier, inc=1, device_id={"lmk": other}, device_id_type=MESH)

    def gather(xf):
        def widen(i, carry):
            load(i).wait()
            for h in range(8):
                rows = pl.ds(i * STEP + h * (STEP // 8), STEP // 8)
                xf[rows, :] = xm[rows, :].astype(F32)
            return carry

        lax.fori_loop(0, steps, widen, 0)

        def pick(i, carry):
            first = pl.multiple_of(i * 32, 32)
            for u in range(32):
                at = ids[first + u] - here * slab
                row = xf[pl.ds(jnp.clip(at, 0, slab - 1), 1), :]
                picked_f[pl.ds(first + u, 1), :] = jnp.where((at >= 0) & (at < slab), row, 0.0)
            return carry

        lax.fori_loop(0, marks // 32, pick, 0)

    pl.run_scoped(gather, pltpu.VMEM((slab, width), F32))
    for g in range(GROUPS):
        picked[g] = picked_f[pl.ds(g * 128, 128), :].astype(BF16)
    pl.semaphore_wait(barrier, 2 * GROUPS - 1)

    def along_pts(src, dst, send, recv, peer):
        return pltpu.make_async_remote_copy(src, dst, send, recv, device_id={"pts": peer}, device_id_type=MESH)

    def along_lmk(src, dst, send, recv, peer):
        return pltpu.make_async_remote_copy(src, dst, send, recv, device_id={"lmk": peer}, device_id_type=MESH)

    for k in range(GROUPS - 1):
        peer = (here + k + 1) % GROUPS
        along_pts(picked.at[peer], rows_in.at[k], c_send.at[0], c_recv.at[0], peer).start()

    def norms_of(low, high):
        def scoped(accs):
            quarter = jnp.full((32, TILE), -0.25, BF16)

            def some(i, carry):
                for h in range(0, PIECES, 4):
                    for q in range(h, h + 4):
                        rows = halves(xm[pl.ds(i * STEP + q * TILE, TILE), :])
                        pltpu.matmul_push_rhs(rows, q // 2 % 2, q % 2, transpose=True)
                        pltpu.matmul_acc_lhs(accs[q % 4], quarter, q // 2 % 2)
                    for q in range(h, h + 4):
                        sq[i, :, pl.ds(q * TILE, TILE)] = pltpu.matmul_pop(accs[q % 4])[:1]
                return carry

            lax.fori_loop(low, high, some, 0)

        pl.run_scoped(scoped, [pltpu.ACC(q % 2)((32, TILE), F32) for q in range(4)])

    norms_of(0, steps // 2)
    along_pts(rows_in, rows_in, c_send.at[0], c_recv.at[0], here).wait_recv()
    total = picked[here].astype(F32)
    for k in range(GROUPS - 1):
        total = total + rows_in[k].astype(F32)
    centers[here] = total.astype(BF16)
    for k in range(GROUPS - 1):
        peer = (here + k + 1) % GROUPS
        along_pts(centers.at[here], centers.at[here], c_send.at[1], c_recv.at[1], peer).start()
    norms_of(steps // 2, steps)
    ct[...] = coef[...].astype(F32).T.astype(BF16)
    pb1[...] = jnp.zeros_like(pb1)
    along_pts(rows_in, rows_in, c_send.at[1], c_recv.at[1], here).wait_recv()
    for g in range(GROUPS):
        rows_f = centers[g].astype(F32)
        ca[pl.ds(g * 128, 128), pl.ds(0, 128)] = (0.5 * rows_f).astype(BF16)
        ca[pl.ds(g * 128, 128), pl.ds(128, 128)] = augment(rows_f)

    def copy1(b):
        mine = part.at[pl.ds(2 + b * PIECES + (1 - core) * GROUPS, GROUPS)]
        return along_lmk(mine, p1r.at[b], s1.at[b], r1.at[b], other)

    def copy4(b):
        half = fit.at[b, pl.ds(core * GROUPS, GROUPS)]
        return along_lmk(half, half, s4.at[b], r4.at[b], other)

    def all2(b):
        return along_lmk(p2r.at[b], p2r.at[b], s2.at[b], r2.at[b], other)

    def all3(b):
        return along_lmk(p2r.at[b], p2r.at[b], s3.at[b], r3.at[b], other)

    def send1(b):
        copy1(b).start()

    def send2(b):
        copy1(b).wait_recv()
        for g in range(GROUPS):
            own = part[2 + b * PIECES + core * GROUPS + g]
            p2s[b, g] = (own.astype(F32) + p1r[b, g].astype(F32)).astype(BF16)
        for k in range(GROUPS - 1):
            peer = (chip + k + 1) % GROUPS
            along_lmk(p2s.at[b, peer], p2r.at[b, k], s2.at[b], r2.at[b], peer * 2 + core).start()

    def send3(b):
        all2(b).wait_recv()
        total = p2s[b, chip].astype(F32)
        for k in range(GROUPS - 1):
            total = total + p2r[b, k].astype(F32)
        mine = core * GROUPS + chip
        fit[b, mine] = total.astype(BF16)
        for k in range(GROUPS - 1):
            peer = (chip + k + 1) % GROUPS
            along_lmk(fit.at[b, mine], fit.at[b, mine], s3.at[b], r3.at[b], peer * 2 + core).start()

    def send4(b):
        all3(b).wait_recv()
        copy4(b).start()

    lane = lax.broadcasted_iota(jnp.int32, (TILE, 128), 1)
    ones = jnp.where(lane < 3, 1.0, 0.0).astype(BF16)
    blank = jnp.zeros((TILE - outs, TILE), BF16)
    segs = marks // SEG

    def main(accs, kts):
        def push_points(unit, m, reg):
            at = pl.multiple_of((unit * 2 + m) * TILE, TILE)
            rows = jnp.concatenate([xm[pl.ds(at, TILE), :], ones], axis=1)
            pltpu.matmul_push_rhs(rows, reg, m, transpose=True)

        def push_tile(par, m, q, reg):
            pltpu.matmul_push_rhs(pb[par][m, pl.ds(q * TILE, TILE), :], reg, m)

        def push_fitted(b, i, c, m, reg):
            pltpu.matmul_push_rhs(jnp.concatenate([fit[b, i * 2 + c], blank], axis=0), reg, m, transpose=True)

        def first_product(unit, par, m, q, reg):
            acc = accs[m]["B"]
            pltpu.matmul_acc_lhs(acc, ct[:, pl.ds(q * TILE, TILE)], reg)
            if q == 3:
                part[unit * 2 + m] = pltpu.matmul_pop(acc).astype(BF16)

        def second_product(kt, i, c, m, reg):
            pltpu.matmul_acc_lhs(accs[m]["C"], kt[i, c, pl.ds(m * (marks // 2), marks // 2), :], reg)

        def unit_step(t, i, par, second):
            kt, old = kts[t % SLOTS], kts[(t - LAG) % SLOTS]
            unit = t * UNITS + i
            after = jnp.minimum(unit + 1, steps * UNITS - 1)
            norms = [sq[t, :, pl.ds(pl.multiple_of((i * 2 + m) * TILE, TILE), TILE)] for m in MXUS]

            def finish(m, s):
                tile = jnp.exp(pltpu.matmul_pop(accs[m]["A"][s % RING]) + norms[m]).astype(BF16)
                rows = pl.ds(s * SEG, SEG)
                kt[i, m, rows, :] = tile
                pb[par][m, rows, :] = tile

            def distances(m, low, high):
                for s in range(low, high):
                    if s >= RING:
                        finish(m, s - RING)
                    acc = accs[m]["A"][s % RING]
                    pltpu.matmul_acc_lhs(acc, ca[pl.ds(s * SEG, SEG), :], 0 if s == low else None)

            def tail():
                for s in range(segs - RING, segs):
                    for m in MXUS:
                        finish(m, s)

            def each(f, *args):
                for m in MXUS:
                    f(*(m if a is MXUS else a for a in args))

            each(distances, MXUS, 0, segs // 2 if second else segs)
            if second:
                b = t - LAG
                each(push_fitted, b, i, 0, MXUS, 0)
                each(first_product, unit, par, MXUS, 0, 1)
                each(push_tile, 1 - par, MXUS, 1, 1)
                each(second_product, old, i, 0, MXUS, 0)
                each(push_points, unit, MXUS, 0)
                each(first_product, unit, par, MXUS, 1, 1)
                each(push_tile, 1 - par, MXUS, 2, 1)
                each(distances, MXUS, segs // 2, segs)
                each(push_fitted, b, i, 1, MXUS, 0)
                each(first_product, unit, par, MXUS, 2, 1)
                each(push_tile, 1 - par, MXUS, 3, 1)
                each(second_product, old, i, 1, MXUS, 0)
                tail()
                each(push_points, after, MXUS, 0)
                each(first_product, unit, par, MXUS, 3, 1)
                each(push_tile, par, MXUS, 0, 1)
            else:
                each(push_tile, 1 - par, MXUS, 1, 0)
                each(first_product, unit, par, MXUS, 0, 1)
                each(push_tile, 1 - par, MXUS, 2, 1)
                each(first_product, unit, par, MXUS, 1, 0)
                each(push_tile, 1 - par, MXUS, 3, 0)
                each(first_product, unit, par, MXUS, 2, 1)
                tail()
                each(push_tile, par, MXUS, 0, 1)
                each(first_product, unit, par, MXUS, 3, 0)
                each(push_points, after, MXUS, 0)

        for m in MXUS:
            push_points(0, m, 0)
            push_tile(1, m, 0, 1)

        for t in range(steps):
            if t >= LAG:
                copy4(t - LAG).wait_recv()

            def pair(i, carry, t=t):
                if t >= 1:

                    @pl.when(i == 1)
                    def _():
                        send1(t - 1)
                        if t >= 2:
                            send3(t - 2)

                    @pl.when(i == 3)
                    def _():
                        send2(t - 1)
                        if t >= 2:
                            send4(t - 2)

                unit_step(t, i * 2, 0, t >= LAG)
                unit_step(t, i * 2 + 1, 1, t >= LAG)
                return carry

            lax.fori_loop(0, UNITS // 2, pair, 0)

        last = steps * UNITS
        for m in MXUS:
            pltpu.matmul_acc_lhs(accs[m]["A"][0], ca[pl.ds(0, SEG), :], 0)
            push_tile(1, m, 1, 0)
            first_product(last, 0, m, 0, 1)
            push_tile(1, m, 2, 1)
            first_product(last, 0, m, 1, 0)
            push_tile(1, m, 3, 0)
            first_product(last, 0, m, 2, 1)
            first_product(last, 0, m, 3, 0)
            pltpu.matmul_pop(accs[m]["A"][0])

        def second_only(b, low, high):
            kt = kts[b % SLOTS]
            for m in MXUS:
                push_fitted(b, low, 0, m, 0)
                push_fitted(b, low, 1, m, 1)

            def unit(i, carry):
                for c in range(2):
                    for m in MXUS:
                        second_product(kt, i, c, m, c)
                        push_fitted(b, i + 1, c, m, c)
                return carry

            lax.fori_loop(low, high - 1, unit, 0)
            for c in range(2):
                for m in MXUS:
                    second_product(kt, high - 1, c, m, c)

        b = steps - 1
        send1(b)
        send3(b - 1)
        copy4(b - 2).wait_recv()
        second_only(b - 2, 0, UNITS // 2)
        send2(b)
        send4(b - 1)
        second_only(b - 2, UNITS // 2, UNITS)
        send3(b)
        copy4(b - 1).wait_recv()
        second_only(b - 1, 0, UNITS // 2)
        send4(b)
        second_only(b - 1, UNITS // 2, UNITS)
        copy4(b).wait_recv()
        second_only(b, 0, UNITS)

        for m in MXUS:
            total = pltpu.matmul_pop(accs[m]["C"])
            for g in range(GROUPS // 2):
                prod_t[m * (GROUPS // 2) + g] = total[g * 128 : (g + 1) * 128, :128].T[:outs]

    def acc(m):
        of = pltpu.ACC(m)
        return {"A": [of((SEG, TILE), F32)] * RING, "B": of((outs, TILE), F32), "C": of((marks // 2, TILE), F32)}

    kt = pltpu.VMEM((UNITS, 2, marks, TILE), BF16)
    pl.run_scoped(main, [acc(m) for m in MXUS], [kt] * SLOTS)

    for k in range(GROUPS - 1):
        peer = (here + k + 1) % GROUPS
        along_pts(prod_t.at[peer], prod_in.at[k], o_send, o_recv, peer).start()

    def sent(b, carry):
        copy1(b).wait_send()
        all2(b).wait_send()
        all3(b).wait_send()
        copy4(b).wait_send()
        return carry

    lax.fori_loop(0, steps, sent, 0)
    for i in range(2):
        along_pts(rows_in, rows_in, c_send.at[i], c_recv.at[i], here).wait_send()
    along_pts(prod_in, prod_in, o_send, o_recv, here).wait_recv()
    total = prod_t[here]
    for k in range(GROUPS - 1):
        total = total + prod_in[k]
    out[...] = total.T * (1.0 / (steps * STEP * GROUPS))
    along_pts(prod_in, prod_in, o_send, o_recv, here).wait_send()


def per_device(points, landmark_ids, coefficients):
    pts_rows, width = points.shape
    marks, outs = coefficients.shape
    steps = pts_rows // STEP
    vmem = pl.BlockSpec(memory_space=pltpu.VMEM)
    dma = pltpu.SemaphoreType.DMA
    return pl.pallas_call(
        functools.partial(body, steps),
        out_shape=jax.ShapeDtypeStruct((marks // GROUPS, outs), F32),
        in_specs=[pl.BlockSpec(memory_space=pltpu.SMEM), vmem, pl.BlockSpec(memory_space=pl.ANY)],
        out_specs=vmem,
        scratch_shapes=[
            pltpu.VMEM((pts_rows, width), BF16),
            pltpu.VMEM((steps, 1, STEP), F32),
            pltpu.VMEM((marks, width + 128), BF16),
            pltpu.VMEM((outs, marks), BF16),
            pltpu.VMEM((marks, width), F32),
            pltpu.VMEM((GROUPS, marks // GROUPS, width), BF16),
            pltpu.VMEM((GROUPS - 1, marks // GROUPS, width), BF16),
            pltpu.VMEM((GROUPS, marks // GROUPS, width), BF16),
            pltpu.VMEM((2, marks, TILE), BF16),
            pltpu.VMEM((2, marks, TILE), BF16),
            pltpu.VMEM((2 + steps * PIECES, outs, TILE), BF16),
            pltpu.VMEM((steps, GROUPS, outs, TILE), BF16),
            pltpu.VMEM((steps, GROUPS, outs, TILE), BF16),
            pltpu.VMEM((steps, GROUPS - 1, outs, TILE), BF16),
            pltpu.VMEM((steps, PIECES, outs, TILE), BF16),
            pltpu.VMEM((GROUPS, outs, 128), F32),
            pltpu.VMEM((GROUPS - 1, outs, 128), F32),
            dma((steps,)),
            dma((2,)),
            dma((2,)),
        ]
        + [dma((steps,))] * 8
        + [dma(()), dma(())],
        compiler_params=pltpu.CompilerParams(collective_id=0, has_side_effects=True, vmem_limit_bytes=60 * 2**20),
    )(landmark_ids, coefficients, points)


def solution(mesh):
    placed = (P("pts", None), P("lmk"), P("lmk", None))
    with jax.sharding.use_abstract_mesh(mesh.abstract_mesh):
        return jax.shard_map(
            per_device, mesh=mesh, in_specs=placed, out_specs=P(("lmk", "pts"), None), check_vma=False
        )
```

```python
import functools

import jax
import jax.numpy as jnp
from jax import lax
from jax.experimental import pallas as pl
from jax.experimental.pallas import tpu as pltpu
from jax.sharding import PartitionSpec as P

MESH = pl.DeviceIdType.MESH
BF16, F32 = jnp.bfloat16, jnp.float32
GROUPS = 8
TILE = 256
UNITS = 8
PIECES = 2 * UNITS
STEP = PIECES * TILE
HALF = UNITS // 2
LAG = 8
SLOTS = LAG + 1
SEG, RING = 128, 3
MXUS = (0, 1)


def augment(rows_f):
    sq = -0.25 * jnp.sum(rows_f * rows_f, axis=1, keepdims=True)
    hi = sq.astype(BF16).astype(F32)
    mid = (sq - hi).astype(BF16).astype(F32)
    low = sq - hi - mid
    lane = lax.broadcasted_iota(jnp.int32, rows_f.shape, 1)
    return jnp.where(lane == 0, hi, jnp.where(lane == 1, mid, jnp.where(lane == 2, low, 0.0))).astype(BF16)


def halves(rows):
    rows_f = rows.astype(F32)
    squares = rows_f * rows_f
    hi = squares.astype(BF16)
    return jnp.concatenate([hi, (squares - hi.astype(F32)).astype(BF16)], axis=1)


def body(steps, ids, coef, points, out, xm, sq, ca, ct, picked_f, picked, rows_in, centers, pb0, pb1, part, p1r, p2s, p2r,
         fit, prod_t, prod_in, load_sem, c_send, c_recv, s1, r1, s2, r2, s3, r3, s4, r4, o_send, o_recv):
    here = lax.axis_index("pts")
    lmk = lax.axis_index("lmk")
    chip, core = lmk // 2, lmk % 2
    other = chip * 2 + 1 - core
    slab, width = xm.shape
    marks = coef.shape[0]
    outs = coef.shape[1]
    pb = (pb0, pb1)

    def load(i):
        rows = pl.ds(i * STEP, STEP)
        return pltpu.make_async_copy(points.at[rows], xm.at[rows], load_sem.at[i])

    def start_load(i, carry):
        load(i).start()
        return carry

    lax.fori_loop(0, steps, start_load, 0)

    barrier = pltpu.get_barrier_semaphore()
    for k in range(GROUPS - 1):
        pl.semaphore_signal(barrier, inc=1, device_id={"pts": (here + k + 1) % GROUPS}, device_id_type=MESH)
        pl.semaphore_signal(barrier, inc=1, device_id={"lmk": ((chip + k + 1) % GROUPS) * 2 + core}, device_id_type=MESH)
    pl.semaphore_signal(barrier, inc=1, device_id={"lmk": other}, device_id_type=MESH)

    def along_pts(src, dst, send, recv, peer):
        return pltpu.make_async_remote_copy(src, dst, send, recv, device_id={"pts": peer}, device_id_type=MESH)

    def along_lmk(src, dst, send, recv, peer):
        return pltpu.make_async_remote_copy(src, dst, send, recv, device_id={"lmk": peer}, device_id_type=MESH)

    def gather(xf):
        def widen(i, carry):
            load(i).wait()
            for h in range(8):
                rows = pl.ds(i * STEP + h * (STEP // 8), STEP // 8)
                xf[rows, :] = xm[rows, :].astype(F32)
            return carry

        lax.fori_loop(0, steps, widen, 0)

        def pick(k, carry):
            peer = (here + k + 1) % GROUPS

            def some(i, carry):
                for u in range(32):
                    row_at = i * 32 + u
                    at = ids[peer * 128 + row_at] - here * slab
                    row = xf[pl.ds(jnp.clip(at, 0, slab - 1), 1), :]
                    picked_f[pl.ds(row_at, 1), :] = jnp.where((at >= 0) & (at < slab), row, 0.0)
                return carry

            lax.fori_loop(0, 4, some, 0)
            picked[peer] = picked_f[...].astype(BF16)

            @pl.when(k < GROUPS - 1)
            def _():
                along_pts(picked.at[peer], rows_in.at[k], c_send.at[0], c_recv.at[0], peer).start()

            return carry

        pl.semaphore_wait(barrier, 2 * GROUPS - 1)
        lax.fori_loop(0, GROUPS, pick, 0)

    pl.run_scoped(gather, pltpu.VMEM((slab, width), F32))

    def norms_of(low, high):
        def scoped(accs):
            quarter = jnp.full((32, TILE), -0.25, BF16)

            def some(i, carry):
                for h in range(0, PIECES, 4):
                    for q in range(h, h + 4):
                        rows = halves(xm[pl.ds(i * STEP + q * TILE, TILE), :])
                        pltpu.matmul_push_rhs(rows, q // 2 % 2, q % 2, transpose=True)
                        pltpu.matmul_acc_lhs(accs[q % 4], quarter, q // 2 % 2)
                    for q in range(h, h + 4):
                        sq[i, pl.ds(q, 1), :] = pltpu.matmul_pop(accs[q % 4])[:1]
                return carry

            lax.fori_loop(low, high, some, 0)

        pl.run_scoped(scoped, [pltpu.ACC(q % 2)((32, TILE), F32) for q in range(4)])

    norms_of(0, steps // 2)
    along_pts(rows_in, rows_in, c_send.at[0], c_recv.at[0], here).wait_recv()
    total = picked[here].astype(F32)
    for k in range(GROUPS - 1):
        total = total + rows_in[k].astype(F32)
    centers[here] = total.astype(BF16)
    for k in range(GROUPS - 1):
        peer = (here + k + 1) % GROUPS
        along_pts(centers.at[here], centers.at[here], c_send.at[1], c_recv.at[1], peer).start()
    norms_of(steps // 2, steps)
    ct[...] = coef[...].astype(F32).T.astype(BF16)
    pb1[...] = jnp.zeros_like(pb1)
    along_pts(rows_in, rows_in, c_send.at[1], c_recv.at[1], here).wait_recv()
    for g in range(GROUPS):
        rows_f = centers[g].astype(F32)
        ca[pl.ds(g * 128, 128), pl.ds(0, 128)] = (0.5 * rows_f).astype(BF16)
        ca[pl.ds(g * 128, 128), pl.ds(128, 128)] = augment(rows_f)

    def copy1(b):
        mine = part.at[pl.ds(2 + b * PIECES + (1 - core) * GROUPS, GROUPS)]
        return along_lmk(mine, p1r.at[b], s1.at[b], r1.at[b], other)

    def copy4(b):
        half = fit.at[b, pl.ds(core * GROUPS, GROUPS)]
        return along_lmk(half, half, s4.at[b], r4.at[b], other)

    def all2(b):
        return along_lmk(p2r.at[b], p2r.at[b], s2.at[b], r2.at[b], other)

    def all3(b):
        return along_lmk(p2r.at[b], p2r.at[b], s3.at[b], r3.at[b], other)

    def send1(b):
        copy1(b).start()

    def send2(b):
        copy1(b).wait_recv()
        for g in range(GROUPS):
            own = part[2 + b * PIECES + core * GROUPS + g]
            p2s[b, g] = (own.astype(F32) + p1r[b, g].astype(F32)).astype(BF16)
        for k in range(GROUPS - 1):
            peer = (chip + k + 1) % GROUPS
            along_lmk(p2s.at[b, peer], p2r.at[b, k], s2.at[b], r2.at[b], peer * 2 + core).start()

    def send3(b):
        all2(b).wait_recv()
        total = p2s[b, chip].astype(F32)
        for k in range(GROUPS - 1):
            total = total + p2r[b, k].astype(F32)
        mine = core * GROUPS + chip
        fit[b, mine] = total.astype(BF16)
        for k in range(GROUPS - 1):
            peer = (chip + k + 1) % GROUPS
            along_lmk(fit.at[b, mine], fit.at[b, mine], s3.at[b], r3.at[b], peer * 2 + core).start()

    def send4(b):
        all3(b).wait_recv()
        copy4(b).start()

    lane = lax.broadcasted_iota(jnp.int32, (TILE, 128), 1)
    ones = jnp.where(lane < 3, 1.0, 0.0).astype(BF16)
    blank = jnp.zeros((TILE - outs, TILE), BF16)
    segs = marks // SEG

    def main(accs, kts):
        def push_points(unit, m, reg):
            at = pl.multiple_of((unit * 2 + m) * TILE, TILE)
            rows = jnp.concatenate([xm[pl.ds(at, TILE), :], ones], axis=1)
            pltpu.matmul_push_rhs(rows, reg, m, transpose=True)

        def push_tile(par, m, q, reg):
            pltpu.matmul_push_rhs(pb[par][m, pl.ds(q * TILE, TILE), :], reg, m)

        def push_fitted(unit, c, m, reg):
            piece = fit[unit // UNITS, unit % UNITS * 2 + c]
            pltpu.matmul_push_rhs(jnp.concatenate([piece, blank], axis=0), reg, m, transpose=True)

        def first_product(unit, par, m, q, reg):
            acc = accs[m]["B"]
            pltpu.matmul_acc_lhs(acc, ct[:, pl.ds(q * TILE, TILE)], reg)
            if q == 3:
                part[unit * 2 + m] = pltpu.matmul_pop(acc).astype(BF16)

        def second_product(kt, i, c, m, reg):
            pltpu.matmul_acc_lhs(accs[m]["C"], kt[i, c, pl.ds(m * (marks // 2), marks // 2), :], reg)

        def unit_step(h, i, par, second):
            kt, old = kts[h % SLOTS], kts[(h - LAG) % SLOTS]
            unit = h * HALF + i
            after = jnp.minimum(unit + 1, steps * UNITS - 1)
            norms = [sq[h // 2, pl.ds((unit % UNITS) * 2 + m, 1), :] for m in MXUS]

            def finish(m, s):
                tile = jnp.exp(pltpu.matmul_pop(accs[m]["A"][s % RING]) + norms[m]).astype(BF16)
                rows = pl.ds(s * SEG, SEG)
                kt[i, m, rows, :] = tile
                pb[par][m, rows, :] = tile

            def distances(m, low, high):
                for s in range(low, high):
                    if s >= RING:
                        finish(m, s - RING)
                    acc = accs[m]["A"][s % RING]
                    pltpu.matmul_acc_lhs(acc, ca[pl.ds(s * SEG, SEG), :], 0 if s == low else None)

            def tail():
                for s in range(segs - RING, segs):
                    for m in MXUS:
                        finish(m, s)

            def each(f, *args):
                for m in MXUS:
                    f(*(m if a is MXUS else a for a in args))

            each(distances, MXUS, 0, segs // 2 if second else segs)
            if second:
                before = unit - LAG * HALF
                each(push_fitted, before, 0, MXUS, 0)
                each(first_product, unit, par, MXUS, 0, 1)
                each(push_tile, 1 - par, MXUS, 1, 1)
                each(second_product, old, i, 0, MXUS, 0)
                each(push_points, unit, MXUS, 0)
                each(first_product, unit, par, MXUS, 1, 1)
                each(push_tile, 1 - par, MXUS, 2, 1)
                each(distances, MXUS, segs // 2, segs)
                each(push_fitted, before, 1, MXUS, 0)
                each(first_product, unit, par, MXUS, 2, 1)
                each(push_tile, 1 - par, MXUS, 3, 1)
                each(second_product, old, i, 1, MXUS, 0)
                tail()
                each(push_points, after, MXUS, 0)
                each(first_product, unit, par, MXUS, 3, 1)
                each(push_tile, par, MXUS, 0, 1)
            else:
                each(push_tile, 1 - par, MXUS, 1, 0)
                each(first_product, unit, par, MXUS, 0, 1)
                each(push_tile, 1 - par, MXUS, 2, 1)
                each(first_product, unit, par, MXUS, 1, 0)
                each(push_tile, 1 - par, MXUS, 3, 0)
                each(first_product, unit, par, MXUS, 2, 1)
                tail()
                each(push_tile, par, MXUS, 0, 1)
                each(first_product, unit, par, MXUS, 3, 0)
                each(push_points, after, MXUS, 0)

        for m in MXUS:
            push_points(0, m, 0)
            push_tile(1, m, 0, 1)

        def exchange(h):
            for stage, behind in ((send2, 3), (send3, 5), (send4, 7)):
                if h % 2 and 0 <= h - behind < 2 * steps:
                    stage((h - behind) // 2)
            if h % 2 == 0 and h >= LAG:
                copy4((h - LAG) // 2).wait_recv()

        for h in range(2 * steps):
            exchange(h)

            def pair(i, carry, h=h):
                if h % 2 == 0 and h >= 2:
                    pl.when(i == 1)(functools.partial(send1, h // 2 - 1))
                unit_step(h, i * 2, 0, h >= LAG)
                unit_step(h, i * 2 + 1, 1, h >= LAG)
                return carry

            lax.fori_loop(0, HALF // 2, pair, 0)

        last = steps * UNITS
        for m in MXUS:
            pltpu.matmul_acc_lhs(accs[m]["A"][0], ca[pl.ds(0, SEG), :], 0)
            push_tile(1, m, 1, 0)
            first_product(last, 0, m, 0, 1)
            push_tile(1, m, 2, 1)
            first_product(last, 0, m, 1, 0)
            push_tile(1, m, 3, 0)
            first_product(last, 0, m, 2, 1)
            first_product(last, 0, m, 3, 0)
            pltpu.matmul_pop(accs[m]["A"][0])

        def second_only(h):
            kt, first = kts[h % SLOTS], h * HALF
            for c in range(2):
                for m in MXUS:
                    push_fitted(first, c, m, c)

            def unit(i, carry):
                for c in range(2):
                    for m in MXUS:
                        second_product(kt, i, c, m, c)
                        push_fitted(first + i + 1, c, m, c)
                return carry

            lax.fori_loop(0, HALF - 1, unit, 0)
            for c in range(2):
                for m in MXUS:
                    second_product(kt, HALF - 1, c, m, c)

        send1(steps - 1)
        for h in range(2 * steps, 2 * steps + LAG):
            exchange(h)
            second_only(h - LAG)

        for m in MXUS:
            total = pltpu.matmul_pop(accs[m]["C"])
            for g in range(GROUPS // 2):
                prod_t[m * (GROUPS // 2) + g] = total[g * 128 : (g + 1) * 128, :128].T[:outs]

    def acc(m):
        of = pltpu.ACC(m)
        return {"A": [of((SEG, TILE), F32)] * RING, "B": of((outs, TILE), F32), "C": of((marks // 2, TILE), F32)}

    kt = pltpu.VMEM((HALF, 2, marks, TILE), BF16)
    pl.run_scoped(main, [acc(m) for m in MXUS], [kt] * SLOTS)

    for k in range(GROUPS - 1):
        peer = (here + k + 1) % GROUPS
        along_pts(prod_t.at[peer], prod_in.at[k], o_send, o_recv, peer).start()

    def sent(b, carry):
        copy1(b).wait_send()
        all2(b).wait_send()
        all3(b).wait_send()
        copy4(b).wait_send()
        return carry

    lax.fori_loop(0, steps, sent, 0)
    for i in range(2):
        along_pts(rows_in, rows_in, c_send.at[i], c_recv.at[i], here).wait_send()
    along_pts(prod_in, prod_in, o_send, o_recv, here).wait_recv()
    total = prod_t[here]
    for k in range(GROUPS - 1):
        total = total + prod_in[k]
    out[...] = total.T * (1.0 / (steps * STEP * GROUPS))
    along_pts(prod_in, prod_in, o_send, o_recv, here).wait_send()


def per_device(points, landmark_ids, coefficients):
    pts_rows, width = points.shape
    marks, outs = coefficients.shape
    steps = pts_rows // STEP
    vmem = pl.BlockSpec(memory_space=pltpu.VMEM)
    dma = pltpu.SemaphoreType.DMA
    return pl.pallas_call(
        functools.partial(body, steps),
        out_shape=jax.ShapeDtypeStruct((marks // GROUPS, outs), F32),
        in_specs=[pl.BlockSpec(memory_space=pltpu.SMEM), vmem, pl.BlockSpec(memory_space=pl.ANY)],
        out_specs=vmem,
        scratch_shapes=[
            pltpu.VMEM((pts_rows, width), BF16),
            pltpu.VMEM((steps, PIECES, TILE), F32),
            pltpu.VMEM((marks, width + 128), BF16),
            pltpu.VMEM((outs, marks), BF16),
            pltpu.VMEM((marks // GROUPS, width), F32),
            pltpu.VMEM((GROUPS, marks // GROUPS, width), BF16),
            pltpu.VMEM((GROUPS - 1, marks // GROUPS, width), BF16),
            pltpu.VMEM((GROUPS, marks // GROUPS, width), BF16),
            pltpu.VMEM((2, marks, TILE), BF16),
            pltpu.VMEM((2, marks, TILE), BF16),
            pltpu.VMEM((2 + steps * PIECES, outs, TILE), BF16),
            pltpu.VMEM((steps, GROUPS, outs, TILE), BF16),
            pltpu.VMEM((steps, GROUPS, outs, TILE), BF16),
            pltpu.VMEM((steps, GROUPS - 1, outs, TILE), BF16),
            pltpu.VMEM((steps, PIECES, outs, TILE), BF16),
            pltpu.VMEM((GROUPS, outs, 128), F32),
            pltpu.VMEM((GROUPS - 1, outs, 128), F32),
            dma((steps,)),
            dma((2,)),
            dma((2,)),
        ]
        + [dma((steps,))] * 8
        + [dma(()), dma(())],
        compiler_params=pltpu.CompilerParams(collective_id=0, has_side_effects=True, vmem_limit_bytes=60 * 2**20),
    )(landmark_ids, coefficients, points)


def solution(mesh):
    placed = (P("pts", None), P("lmk"), P("lmk", None))
    with jax.sharding.use_abstract_mesh(mesh.abstract_mesh):
        return jax.shard_map(
            per_device, mesh=mesh, in_specs=placed, out_specs=P(("lmk", "pts"), None), check_vma=False
        )
```

```python
import functools

import jax
import jax.numpy as jnp
from jax import lax
from jax.experimental import pallas as pl
from jax.experimental.pallas import tpu as pltpu
from jax.sharding import PartitionSpec as P

MESH = pl.DeviceIdType.MESH
BF16, F32 = jnp.bfloat16, jnp.float32
GROUPS = 8
TILE = 256
UNITS = 8
PIECES = 2 * UNITS
STEP = PIECES * TILE
HALF = UNITS // 2
LAG = 8
BACK = LAG * HALF + 1
KEPT = (BACK + 1) // 2
SEG, RING = 128, 3
MXUS = (0, 1)


def augment(rows_f):
    sq = -0.25 * jnp.sum(rows_f * rows_f, axis=1, keepdims=True)
    hi = sq.astype(BF16).astype(F32)
    mid = (sq - hi).astype(BF16).astype(F32)
    low = sq - hi - mid
    lane = lax.broadcasted_iota(jnp.int32, rows_f.shape, 1)
    return jnp.where(lane == 0, hi, jnp.where(lane == 1, mid, jnp.where(lane == 2, low, 0.0))).astype(BF16)


def halves(rows):
    rows_f = rows.astype(F32)
    squares = rows_f * rows_f
    hi = squares.astype(BF16)
    return jnp.concatenate([hi, (squares - hi.astype(F32)).astype(BF16)], axis=1)


def body(steps, ids, ct, points, out, xm, sq, ca, picked_f, picked, rows_in, centers, pb0, pb1, part, p1r, p2s, p2r,
         fit, prod_t, prod_in, load_sem, c_send, c_recv, s1, r1, s2, r2, s3, r3, s4, r4, o_send, o_recv):
    here = lax.axis_index("pts")
    lmk = lax.axis_index("lmk")
    chip, core = lmk // 2, lmk % 2
    other = chip * 2 + 1 - core
    slab, width = xm.shape
    outs, marks = ct.shape
    pb = (pb0, pb1)

    def load(i):
        rows = pl.ds(i * STEP, STEP)
        return pltpu.make_async_copy(points.at[rows], xm.at[rows], load_sem.at[i])

    def start_load(i, carry):
        load(i).start()
        return carry

    lax.fori_loop(0, steps, start_load, 0)

    barrier = pltpu.get_barrier_semaphore()
    for k in range(GROUPS - 1):
        pl.semaphore_signal(barrier, inc=1, device_id={"pts": (here + k + 1) % GROUPS}, device_id_type=MESH)
        pl.semaphore_signal(barrier, inc=1, device_id={"lmk": ((chip + k + 1) % GROUPS) * 2 + core}, device_id_type=MESH)
    pl.semaphore_signal(barrier, inc=1, device_id={"lmk": other}, device_id_type=MESH)

    def along_pts(src, dst, send, recv, peer):
        return pltpu.make_async_remote_copy(src, dst, send, recv, device_id={"pts": peer}, device_id_type=MESH)

    def along_lmk(src, dst, send, recv, peer):
        return pltpu.make_async_remote_copy(src, dst, send, recv, device_id={"lmk": peer}, device_id_type=MESH)

    def gather(xf):
        def widen(i, carry):
            load(i).wait()
            for h in range(8):
                rows = pl.ds(i * STEP + h * (STEP // 8), STEP // 8)
                xf[rows, :] = xm[rows, :].astype(F32)
            return carry

        lax.fori_loop(0, steps, widen, 0)

        def pick(k, carry):
            peer = (here + k + 1) % GROUPS

            def some(i, carry):
                for u in range(32):
                    row_at = i * 32 + u
                    at = ids[peer * 128 + row_at] - here * slab
                    row = xf[pl.ds(jnp.clip(at, 0, slab - 1), 1), :]
                    picked_f[pl.ds(row_at, 1), :] = jnp.where((at >= 0) & (at < slab), row, 0.0)
                return carry

            lax.fori_loop(0, 4, some, 0)
            picked[peer] = picked_f[...].astype(BF16)

            @pl.when(k < GROUPS - 1)
            def _():
                along_pts(picked.at[peer], rows_in.at[k], c_send.at[0], c_recv.at[0], peer).start()

            return carry

        pl.semaphore_wait(barrier, 2 * GROUPS - 1)
        lax.fori_loop(0, GROUPS, pick, 0)

    pl.run_scoped(gather, pltpu.VMEM((slab, width), F32))

    def norms_of(low, high):
        def scoped(accs):
            quarter = jnp.full((32, TILE), -0.25, BF16)

            def some(i, carry):
                for h in range(0, PIECES, 4):
                    for q in range(h, h + 4):
                        rows = halves(xm[pl.ds(i * STEP + q * TILE, TILE), :])
                        pltpu.matmul_push_rhs(rows, q // 2 % 2, q % 2, transpose=True)
                        pltpu.matmul_acc_lhs(accs[q % 4], quarter, q // 2 % 2)
                    for q in range(h, h + 4):
                        sq[i, pl.ds(q, 1), :] = pltpu.matmul_pop(accs[q % 4])[:1]
                return carry

            lax.fori_loop(low, high, some, 0)

        pl.run_scoped(scoped, [pltpu.ACC(q % 2)((32, TILE), F32) for q in range(4)])

    norms_of(0, steps // 2)
    along_pts(rows_in, rows_in, c_send.at[0], c_recv.at[0], here).wait_recv()
    total = picked[here].astype(F32)
    for k in range(GROUPS - 1):
        total = total + rows_in[k].astype(F32)
    centers[here] = total.astype(BF16)
    for k in range(GROUPS - 1):
        peer = (here + k + 1) % GROUPS
        along_pts(centers.at[here], centers.at[here], c_send.at[1], c_recv.at[1], peer).start()
    norms_of(steps // 2, steps)
    pb1[...] = jnp.zeros_like(pb1)
    along_pts(rows_in, rows_in, c_send.at[1], c_recv.at[1], here).wait_recv()
    for g in range(GROUPS):
        rows_f = centers[g].astype(F32)
        ca[pl.ds(g * 128, 128), pl.ds(0, 128)] = (0.5 * rows_f).astype(BF16)
        ca[pl.ds(g * 128, 128), pl.ds(128, 128)] = augment(rows_f)

    def copy1(b):
        mine = part.at[pl.ds(2 + b * PIECES + (1 - core) * GROUPS, GROUPS)]
        return along_lmk(mine, p1r.at[b], s1.at[b], r1.at[b], other)

    def copy4(b):
        half = fit.at[pl.ds(2 + b * PIECES + core * GROUPS, GROUPS)]
        return along_lmk(half, half, s4.at[b], r4.at[b], other)

    def all2(b):
        return along_lmk(p2r.at[b], p2r.at[b], s2.at[b], r2.at[b], other)

    def all3(b):
        return along_lmk(p2r.at[b], p2r.at[b], s3.at[b], r3.at[b], other)

    def send1(b):
        copy1(b).start()

    def send2(b):
        copy1(b).wait_recv()
        for g in range(GROUPS):
            own = part[2 + b * PIECES + core * GROUPS + g]
            p2s[b, g] = (own.astype(F32) + p1r[b, g].astype(F32)).astype(BF16)
        for k in range(GROUPS - 1):
            peer = (chip + k + 1) % GROUPS
            along_lmk(p2s.at[b, peer], p2r.at[b, k], s2.at[b], r2.at[b], peer * 2 + core).start()

    def send3(b):
        all2(b).wait_recv()
        total = p2s[b, chip].astype(F32)
        for k in range(GROUPS - 1):
            total = total + p2r[b, k].astype(F32)
        mine = 2 + b * PIECES + core * GROUPS + chip
        fit[mine] = total.astype(BF16)
        for k in range(GROUPS - 1):
            peer = (chip + k + 1) % GROUPS
            along_lmk(fit.at[mine], fit.at[mine], s3.at[b], r3.at[b], peer * 2 + core).start()

    def send4(b):
        all3(b).wait_recv()
        copy4(b).start()

    lane = lax.broadcasted_iota(jnp.int32, (TILE, 128), 1)
    ones = jnp.where(lane < 3, 1.0, 0.0).astype(BF16)
    blank = jnp.zeros((TILE - outs, TILE), BF16)
    segs = marks // SEG

    def main(accs, kts):
        def push_points(unit, m, reg):
            at = pl.multiple_of((unit * 2 + m) * TILE, TILE)
            rows = jnp.concatenate([xm[pl.ds(at, TILE), :], ones], axis=1)
            pltpu.matmul_push_rhs(rows, reg, m, transpose=True)

        def push_tile(par, m, q, reg):
            pltpu.matmul_push_rhs(pb[par][m, pl.ds(q * TILE, TILE), :], reg, m)

        def push_fitted(unit, c, m, reg):
            pltpu.matmul_push_rhs(jnp.concatenate([fit[2 + unit * 2 + c], blank], axis=0), reg, m, transpose=True)

        def first_product(unit, par, m, q, reg):
            acc = accs[m]["B"]
            pltpu.matmul_acc_lhs(acc, ct[:, pl.ds(q * TILE, TILE)], reg)
            if q == 3:
                part[unit * 2 + m] = pltpu.matmul_pop(acc).astype(BF16)

        def second_product(unit, par, c, m, reg):
            tile = kts[par][lax.rem(unit // 2 + KEPT, KEPT), c, pl.ds(m * (marks // 2), marks // 2), :]
            pltpu.matmul_acc_lhs(accs[m]["C"], tile, reg)

        def unit_step(h, i, par, second):
            unit = h * HALF + i
            slot = lax.rem(unit // 2, KEPT)
            after = jnp.minimum(unit + 1, steps * UNITS - 1)
            norms = [sq[unit // UNITS, pl.ds((unit % UNITS) * 2 + m, 1), :] for m in MXUS]

            def finish(m, s):
                tile = jnp.exp(pltpu.matmul_pop(accs[m]["A"][s % RING]) + norms[m]).astype(BF16)
                rows = pl.ds(s * SEG, SEG)
                kts[par][slot, m, rows, :] = tile
                pb[par][m, rows, :] = tile

            def distances(m, low, high):
                for s in range(low, high):
                    if s >= RING:
                        finish(m, s - RING)
                    acc = accs[m]["A"][s % RING]
                    pltpu.matmul_acc_lhs(acc, ca[pl.ds(s * SEG, SEG), :], 0 if s == low else None)

            def tail():
                for s in range(segs - RING, segs):
                    for m in MXUS:
                        finish(m, s)

            def each(f, *args):
                for m in MXUS:
                    f(*(m if a is MXUS else a for a in args))

            each(distances, MXUS, 0, segs // 2 if second else segs)
            if second:
                before = unit - BACK
                each(push_fitted, before, 0, MXUS, 0)
                each(first_product, unit, par, MXUS, 0, 1)
                each(push_tile, 1 - par, MXUS, 1, 1)
                each(second_product, before, 1 - par, 0, MXUS, 0)
                each(push_points, unit, MXUS, 0)
                each(first_product, unit, par, MXUS, 1, 1)
                each(push_tile, 1 - par, MXUS, 2, 1)
                each(distances, MXUS, segs // 2, segs)
                each(push_fitted, before, 1, MXUS, 0)
                each(first_product, unit, par, MXUS, 2, 1)
                each(push_tile, 1 - par, MXUS, 3, 1)
                each(second_product, before, 1 - par, 1, MXUS, 0)
                tail()
                each(push_points, after, MXUS, 0)
                each(first_product, unit, par, MXUS, 3, 1)
                each(push_tile, par, MXUS, 0, 1)
            else:
                each(push_tile, 1 - par, MXUS, 1, 0)
                each(first_product, unit, par, MXUS, 0, 1)
                each(push_tile, 1 - par, MXUS, 2, 1)
                each(first_product, unit, par, MXUS, 1, 0)
                each(push_tile, 1 - par, MXUS, 3, 0)
                each(first_product, unit, par, MXUS, 2, 1)
                tail()
                each(push_tile, par, MXUS, 0, 1)
                each(first_product, unit, par, MXUS, 3, 0)
                each(push_points, after, MXUS, 0)

        for m in MXUS:
            push_points(0, m, 0)
            push_tile(1, m, 0, 1)

        def exchange(h):
            for stage, behind in ((send2, 3), (send3, 5), (send4, 7)):
                due = (h % 2 == 1) & (h >= behind) & (h < behind + 2 * steps)
                pl.when(due)(functools.partial(stage, (h - behind) // 2))

        def tiles(low, high, second):
            def half(h, carry):
                exchange(h)
                if second:
                    pl.when(h % 2 == 0)(lambda: copy4((h - LAG) // 2).wait_recv())

                def pair(i, carry):
                    pl.when((i == 1) & (h % 2 == 0) & (h >= 2))(functools.partial(send1, h // 2 - 1))
                    unit_step(h, i * 2, 0, second)
                    unit_step(h, i * 2 + 1, 1, second)
                    return carry

                return lax.fori_loop(0, HALF // 2, pair, carry)

            lax.fori_loop(low, high, half, 0)

        kts[1][KEPT - 1] = jnp.zeros((2, marks, TILE), BF16)
        fit[pl.ds(0, 2)] = jnp.zeros((2, outs, TILE), BF16)
        tiles(0, LAG, False)
        tiles(LAG, 2 * steps, True)

        def second_only(first, count):
            turns = [(first + i, (count + i) % 2, c) for i in range(count) for c in range(2)]
            for unit, _, c in turns[:2]:
                for m in MXUS:
                    push_fitted(unit, c, m, c)
            for at, (unit, par, c) in enumerate(turns):
                for m in MXUS:
                    second_product(unit, par, c, m, c)
                    if at + 2 < len(turns):
                        push_fitted(turns[at + 2][0], c, m, c)

        last = steps * UNITS
        for m in MXUS:
            pltpu.matmul_acc_lhs(accs[m]["A"][0], ca[pl.ds(0, SEG), :], 0)
            push_tile(1, m, 1, 0)
            first_product(last, 0, m, 0, 1)
            push_tile(1, m, 2, 1)
            first_product(last, 0, m, 1, 0)
            push_tile(1, m, 3, 0)
            first_product(last, 0, m, 2, 1)
            first_product(last, 0, m, 3, 0)
            pltpu.matmul_pop(accs[m]["A"][0])

        def rest(h, carry):
            exchange(h)
            pl.when(h % 2 == 0)(lambda: copy4((h - LAG) // 2).wait_recv())
            second_only((h - LAG) * HALF, HALF)
            return carry

        send1(steps - 1)
        second_only((2 * steps - LAG) * HALF - 1, 1)
        lax.fori_loop(2 * steps, 2 * steps + LAG, rest, 0)

        for m in MXUS:
            total = pltpu.matmul_pop(accs[m]["C"])
            for g in range(GROUPS // 2):
                prod_t[m * (GROUPS // 2) + g] = total[g * 128 : (g + 1) * 128, :128].T[:outs]

    def acc(m):
        of = pltpu.ACC(m)
        return {"A": [of((SEG, TILE), F32)] * RING, "B": of((outs, TILE), F32), "C": of((marks // 2, TILE), F32)}

    pl.run_scoped(main, [acc(m) for m in MXUS], [pltpu.VMEM((KEPT, 2, marks, TILE), BF16)] * 2)

    for k in range(GROUPS - 1):
        peer = (here + k + 1) % GROUPS
        along_pts(prod_t.at[peer], prod_in.at[k], o_send, o_recv, peer).start()

    def sent(b, carry):
        copy1(b).wait_send()
        all2(b).wait_send()
        all3(b).wait_send()
        copy4(b).wait_send()
        return carry

    lax.fori_loop(0, steps, sent, 0)
    for i in range(2):
        along_pts(rows_in, rows_in, c_send.at[i], c_recv.at[i], here).wait_send()
    along_pts(prod_in, prod_in, o_send, o_recv, here).wait_recv()
    total = prod_t[here]
    for k in range(GROUPS - 1):
        total = total + prod_in[k]
    out[...] = total
    along_pts(prod_in, prod_in, o_send, o_recv, here).wait_send()


def per_device(points, landmark_ids, coefficients):
    pts_rows, width = points.shape
    marks, outs = coefficients.shape
    steps = pts_rows // STEP
    vmem = pl.BlockSpec(memory_space=pltpu.VMEM)
    dma = pltpu.SemaphoreType.DMA
    product = pl.pallas_call(
        functools.partial(body, steps),
        out_shape=jax.ShapeDtypeStruct((outs, marks // GROUPS), F32),
        in_specs=[pl.BlockSpec(memory_space=pltpu.SMEM), vmem, pl.BlockSpec(memory_space=pl.ANY)],
        out_specs=vmem,
        scratch_shapes=[
            pltpu.VMEM((pts_rows, width), BF16),
            pltpu.VMEM((steps, PIECES, TILE), F32),
            pltpu.VMEM((marks, width + 128), BF16),
            pltpu.VMEM((marks // GROUPS, width), F32),
            pltpu.VMEM((GROUPS, marks // GROUPS, width), BF16),
            pltpu.VMEM((GROUPS - 1, marks // GROUPS, width), BF16),
            pltpu.VMEM((GROUPS, marks // GROUPS, width), BF16),
            pltpu.VMEM((2, marks, TILE), BF16),
            pltpu.VMEM((2, marks, TILE), BF16),
            pltpu.VMEM((2 + steps * PIECES, outs, TILE), BF16),
            pltpu.VMEM((steps, GROUPS, outs, TILE), BF16),
            pltpu.VMEM((steps, GROUPS, outs, TILE), BF16),
            pltpu.VMEM((steps, GROUPS - 1, outs, TILE), BF16),
            pltpu.VMEM((2 + steps * PIECES, outs, TILE), BF16),
            pltpu.VMEM((GROUPS, outs, 128), F32),
            pltpu.VMEM((GROUPS - 1, outs, 128), F32),
            dma((steps,)),
            dma((2,)),
            dma((2,)),
        ]
        + [dma((steps,))] * 8
        + [dma(()), dma(())],
        compiler_params=pltpu.CompilerParams(collective_id=0, has_side_effects=True, vmem_limit_bytes=60 * 2**20),
    )(landmark_ids, coefficients.T, points)
    return product.T / (pts_rows * GROUPS)


def solution(mesh):
    placed = (P("pts", None), P("lmk"), P("lmk", None))
    with jax.sharding.use_abstract_mesh(mesh.abstract_mesh):
        return jax.shard_map(
            per_device, mesh=mesh, in_specs=placed, out_specs=P(("lmk", "pts"), None), check_vma=False
        )
```

```python
import functools

import jax
import jax.numpy as jnp
from jax import lax
from jax.experimental import pallas as pl
from jax.experimental.pallas import tpu as pltpu
from jax.sharding import PartitionSpec as P

MESH = pl.DeviceIdType.MESH
BF16, F32 = jnp.bfloat16, jnp.float32
GROUPS = 8
TILE = 256
UNITS = 8
PIECES = 2 * UNITS
STEP = PIECES * TILE
HALF = UNITS // 2
LAG = 8
BACK = LAG * HALF + 3
KEPT = (BACK + 1) // 2
BLANK = 2 * (BACK - LAG * HALF)
SEG, RING = 128, 3
MXUS = (0, 1)


def augment(rows_f):
    sq = -0.25 * jnp.sum(rows_f * rows_f, axis=1, keepdims=True)
    hi = sq.astype(BF16).astype(F32)
    mid = (sq - hi).astype(BF16).astype(F32)
    low = sq - hi - mid
    lane = lax.broadcasted_iota(jnp.int32, rows_f.shape, 1)
    return jnp.where(lane == 0, hi, jnp.where(lane == 1, mid, jnp.where(lane == 2, low, 0.0))).astype(BF16)


def halves(rows):
    rows_f = rows.astype(F32)
    squares = rows_f * rows_f
    hi = squares.astype(BF16)
    return jnp.concatenate([hi, (squares - hi.astype(F32)).astype(BF16)], axis=1)


def body(steps, ids, ct, points, out, xm, sq, ca, picked_f, picked, rows_in, centers, pb0, pb1, part, p1r, p2s, p2r,
         fit, prod_t, prod_in, load_sem, c_send, c_recv, s1, r1, s2, r2, s3, r3, s4, r4, o_send, o_recv):
    here = lax.axis_index("pts")
    lmk = lax.axis_index("lmk")
    chip, core = lmk // 2, lmk % 2
    other = chip * 2 + 1 - core
    slab, width = xm.shape
    outs, marks = ct.shape
    pb = (pb0, pb1)

    def load(i):
        rows = pl.ds(i * STEP, STEP)
        return pltpu.make_async_copy(points.at[rows], xm.at[rows], load_sem.at[i])

    def start_load(i, carry):
        load(i).start()
        return carry

    lax.fori_loop(0, steps, start_load, 0)

    barrier = pltpu.get_barrier_semaphore()
    for k in range(GROUPS - 1):
        pl.semaphore_signal(barrier, inc=1, device_id={"pts": (here + k + 1) % GROUPS}, device_id_type=MESH)
        pl.semaphore_signal(barrier, inc=1, device_id={"lmk": ((chip + k + 1) % GROUPS) * 2 + core}, device_id_type=MESH)
    pl.semaphore_signal(barrier, inc=1, device_id={"lmk": other}, device_id_type=MESH)

    def along_pts(src, dst, send, recv, peer):
        return pltpu.make_async_remote_copy(src, dst, send, recv, device_id={"pts": peer}, device_id_type=MESH)

    def along_lmk(src, dst, send, recv, peer):
        return pltpu.make_async_remote_copy(src, dst, send, recv, device_id={"lmk": peer}, device_id_type=MESH)

    def gather(xf):
        def widen(i, carry):
            load(i).wait()
            for h in range(8):
                rows = pl.ds(i * STEP + h * (STEP // 8), STEP // 8)
                xf[rows, :] = xm[rows, :].astype(F32)
            return carry

        lax.fori_loop(0, steps, widen, 0)

        def pick(k, carry):
            peer = (here + k + 1) % GROUPS

            def some(i, carry):
                for u in range(32):
                    row_at = i * 32 + u
                    at = ids[peer * 128 + row_at] - here * slab
                    row = xf[pl.ds(jnp.clip(at, 0, slab - 1), 1), :]
                    picked_f[pl.ds(row_at, 1), :] = jnp.where((at >= 0) & (at < slab), row, 0.0)
                return carry

            lax.fori_loop(0, 4, some, 0)
            picked[peer] = picked_f[...].astype(BF16)

            @pl.when(k < GROUPS - 1)
            def _():
                along_pts(picked.at[peer], rows_in.at[k], c_send.at[0], c_recv.at[0], peer).start()

            return carry

        pl.semaphore_wait(barrier, 2 * GROUPS - 1)
        lax.fori_loop(0, GROUPS, pick, 0)

    pl.run_scoped(gather, pltpu.VMEM((slab, width), F32))

    def norms_of(low, high):
        def scoped(accs):
            quarter = jnp.full((32, TILE), -0.25, BF16)

            def some(i, carry):
                for h in range(0, PIECES, 4):
                    for q in range(h, h + 4):
                        rows = halves(xm[pl.ds(i * STEP + q * TILE, TILE), :])
                        pltpu.matmul_push_rhs(rows, q // 2 % 2, q % 2, transpose=True)
                        pltpu.matmul_acc_lhs(accs[q % 4], quarter, q // 2 % 2)
                    for q in range(h, h + 4):
                        sq[i, pl.ds(q, 1), :] = pltpu.matmul_pop(accs[q % 4])[:1]
                return carry

            lax.fori_loop(low, high, some, 0)

        pl.run_scoped(scoped, [pltpu.ACC(q % 2)((32, TILE), F32) for q in range(4)])

    norms_of(0, steps // 2)
    along_pts(rows_in, rows_in, c_send.at[0], c_recv.at[0], here).wait_recv()
    total = picked[here].astype(F32)
    for k in range(GROUPS - 1):
        total = total + rows_in[k].astype(F32)
    centers[here] = total.astype(BF16)
    for k in range(GROUPS - 1):
        peer = (here + k + 1) % GROUPS
        along_pts(centers.at[here], centers.at[here], c_send.at[1], c_recv.at[1], peer).start()
    norms_of(steps // 2, steps)
    pb1[...] = jnp.zeros_like(pb1)
    along_pts(rows_in, rows_in, c_send.at[1], c_recv.at[1], here).wait_recv()
    for g in range(GROUPS):
        rows_f = centers[g].astype(F32)
        ca[pl.ds(g * 128, 128), pl.ds(0, 128)] = (0.5 * rows_f).astype(BF16)
        ca[pl.ds(g * 128, 128), pl.ds(128, 128)] = augment(rows_f)

    def copy1(b):
        mine = part.at[pl.ds(2 + b * PIECES + (1 - core) * GROUPS, GROUPS)]
        return along_lmk(mine, p1r.at[b], s1.at[b], r1.at[b], other)

    def copy4(b):
        half = fit.at[pl.ds(BLANK + b * PIECES + core * GROUPS, GROUPS)]
        return along_lmk(half, half, s4.at[b], r4.at[b], other)

    def all2(b):
        return along_lmk(p2r.at[b], p2r.at[b], s2.at[b], r2.at[b], other)

    def all3(b):
        return along_lmk(p2r.at[b], p2r.at[b], s3.at[b], r3.at[b], other)

    def send1(b):
        copy1(b).start()

    def send2(b):
        copy1(b).wait_recv()
        for g in range(GROUPS):
            own = part[2 + b * PIECES + core * GROUPS + g]
            p2s[b, g] = (own.astype(F32) + p1r[b, g].astype(F32)).astype(BF16)
        for k in range(GROUPS - 1):
            peer = (chip + k + 1) % GROUPS
            along_lmk(p2s.at[b, peer], p2r.at[b, k], s2.at[b], r2.at[b], peer * 2 + core).start()

    def send3(b):
        all2(b).wait_recv()
        total = p2s[b, chip].astype(F32)
        for k in range(GROUPS - 1):
            total = total + p2r[b, k].astype(F32)
        mine = BLANK + b * PIECES + core * GROUPS + chip
        fit[mine] = total.astype(BF16)
        for k in range(GROUPS - 1):
            peer = (chip + k + 1) % GROUPS
            along_lmk(fit.at[mine], fit.at[mine], s3.at[b], r3.at[b], peer * 2 + core).start()

    def send4(b):
        all3(b).wait_recv()
        copy4(b).start()

    lane = lax.broadcasted_iota(jnp.int32, (TILE, 128), 1)
    ones = jnp.where(lane < 3, 1.0, 0.0).astype(BF16)
    blank = jnp.zeros((TILE - outs, TILE), BF16)
    segs = marks // SEG

    def main(accs, kts):
        def push_points(unit, m, reg):
            at = pl.multiple_of((unit * 2 + m) * TILE, TILE)
            rows = jnp.concatenate([xm[pl.ds(at, TILE), :], ones], axis=1)
            pltpu.matmul_push_rhs(rows, reg, m, transpose=True)

        def push_tile(par, m, q, reg):
            pltpu.matmul_push_rhs(pb[par][m, pl.ds(q * TILE, TILE), :], reg, m)

        def push_fitted(unit, c, m, reg):
            pltpu.matmul_push_rhs(jnp.concatenate([fit[BLANK + unit * 2 + c], blank], axis=0), reg, m, transpose=True)

        def first_product(unit, par, m, q, reg):
            acc = accs[m]["B"]
            pltpu.matmul_acc_lhs(acc, ct[:, pl.ds(q * TILE, TILE)], reg)
            if q == 3:
                part[unit * 2 + m] = pltpu.matmul_pop(acc).astype(BF16)

        def second_product(unit, par, c, m, reg):
            tile = kts[par][lax.rem(unit // 2 + KEPT, KEPT), c, pl.ds(m * (marks // 2), marks // 2), :]
            pltpu.matmul_acc_lhs(accs[m]["C"], tile, reg)

        def unit_step(h, i, par, second):
            unit = h * HALF + i
            slot = lax.rem(unit // 2, KEPT)
            after = jnp.minimum(unit + 1, steps * UNITS - 1)
            norms = [sq[unit // UNITS, pl.ds((unit % UNITS) * 2 + m, 1), :] for m in MXUS]

            def finish(m, s):
                tile = jnp.exp(pltpu.matmul_pop(accs[m]["A"][s % RING]) + norms[m]).astype(BF16)
                rows = pl.ds(s * SEG, SEG)
                kts[par][slot, m, rows, :] = tile
                pb[par][m, rows, :] = tile

            def distances(m, low, high):
                for s in range(low, high):
                    if s >= RING:
                        finish(m, s - RING)
                    acc = accs[m]["A"][s % RING]
                    pltpu.matmul_acc_lhs(acc, ca[pl.ds(s * SEG, SEG), :], 0 if s == low else None)

            def tail():
                for s in range(segs - RING, segs):
                    for m in MXUS:
                        finish(m, s)

            def each(f, *args):
                for m in MXUS:
                    f(*(m if a is MXUS else a for a in args))

            each(distances, MXUS, 0, segs // 2 if second else 3)
            if second:
                before = unit - BACK
                each(push_fitted, before, 0, MXUS, 0)
                each(first_product, unit, par, MXUS, 0, 1)
                each(push_tile, 1 - par, MXUS, 1, 1)
                each(second_product, before, 1 - par, 0, MXUS, 0)
                each(push_points, unit, MXUS, 0)
                each(first_product, unit, par, MXUS, 1, 1)
                each(push_tile, 1 - par, MXUS, 2, 1)
                each(distances, MXUS, segs // 2, segs)
                each(push_fitted, before, 1, MXUS, 0)
                each(first_product, unit, par, MXUS, 2, 1)
                each(push_tile, 1 - par, MXUS, 3, 1)
                each(second_product, before, 1 - par, 1, MXUS, 0)
                tail()
                each(push_points, after, MXUS, 0)
                each(first_product, unit, par, MXUS, 3, 1)
                each(push_tile, par, MXUS, 0, 1)
            else:
                each(push_points, unit, MXUS, 0)
                each(first_product, unit, par, MXUS, 0, 1)
                each(push_tile, 1 - par, MXUS, 1, 1)
                each(distances, MXUS, 3, 6)
                each(push_points, unit, MXUS, 0)
                each(first_product, unit, par, MXUS, 1, 1)
                each(push_tile, 1 - par, MXUS, 2, 1)
                each(distances, MXUS, 6, segs)
                each(push_tile, 1 - par, MXUS, 3, 0)
                each(first_product, unit, par, MXUS, 2, 1)
                tail()
                each(push_tile, par, MXUS, 0, 1)
                each(first_product, unit, par, MXUS, 3, 0)
                each(push_points, after, MXUS, 0)

        for m in MXUS:
            push_points(0, m, 0)
            push_tile(1, m, 0, 1)

        def exchange(h):
            for stage, behind in ((send2, 3), (send3, 5), (send4, 7)):
                due = (h % 2 == 1) & (h >= behind) & (h < behind + 2 * steps)
                pl.when(due)(functools.partial(stage, (h - behind) // 2))

        def tiles(low, high, second):
            def half(h, carry):
                def pair(i, carry):
                    @pl.when(i == 1)
                    def _():
                        pl.when((h % 2 == 0) & (h >= 2))(functools.partial(send1, h // 2 - 1))
                        exchange(h)
                        if second:
                            pl.when(h % 2 == 0)(lambda: copy4((h - LAG) // 2).wait_recv())

                    unit_step(h, i * 2, 0, second)
                    unit_step(h, i * 2 + 1, 1, second)
                    return carry

                return lax.fori_loop(0, HALF // 2, pair, carry)

            lax.fori_loop(low, high, half, 0)

        for unit in range(LAG * HALF - BACK, 0):
            kts[unit % 2][unit // 2 + KEPT] = jnp.zeros((2, marks, TILE), BF16)
        fit[pl.ds(0, BLANK)] = jnp.zeros((BLANK, outs, TILE), BF16)
        tiles(0, LAG, False)
        tiles(LAG, 2 * steps, True)

        def second_only(first, count):
            turns = [(first + i, (count + i) % 2, c) for i in range(count) for c in range(2)]
            for unit, _, c in turns[:2]:
                for m in MXUS:
                    push_fitted(unit, c, m, c)
            for at, (unit, par, c) in enumerate(turns):
                for m in MXUS:
                    second_product(unit, par, c, m, c)
                    if at + 2 < len(turns):
                        push_fitted(turns[at + 2][0], c, m, c)

        last = steps * UNITS
        for m in MXUS:
            pltpu.matmul_acc_lhs(accs[m]["A"][0], ca[pl.ds(0, SEG), :], 0)
            push_tile(1, m, 1, 0)
            first_product(last, 0, m, 0, 1)
            push_tile(1, m, 2, 1)
            first_product(last, 0, m, 1, 0)
            push_tile(1, m, 3, 0)
            first_product(last, 0, m, 2, 1)
            first_product(last, 0, m, 3, 0)
            pltpu.matmul_pop(accs[m]["A"][0])

        def rest(h, carry):
            exchange(h)
            pl.when(h % 2 == 0)(lambda: copy4((h - LAG) // 2).wait_recv())
            second_only((h - LAG) * HALF, HALF)
            return carry

        send1(steps - 1)
        ahead = BACK - LAG * HALF
        second_only((2 * steps - LAG) * HALF - ahead, ahead)
        lax.fori_loop(2 * steps, 2 * steps + LAG, rest, 0)

        for m in MXUS:
            total = pltpu.matmul_pop(accs[m]["C"])
            for g in range(GROUPS // 2):
                prod_t[m * (GROUPS // 2) + g] = total[g * 128 : (g + 1) * 128, :128].T[:outs]

    def acc(m):
        of = pltpu.ACC(m)
        return {"A": [of((SEG, TILE), F32)] * RING, "B": of((outs, TILE), F32), "C": of((marks // 2, TILE), F32)}

    pl.run_scoped(main, [acc(m) for m in MXUS], [pltpu.VMEM((KEPT, 2, marks, TILE), BF16)] * 2)

    for k in range(GROUPS - 1):
        peer = (here + k + 1) % GROUPS
        along_pts(prod_t.at[peer], prod_in.at[k], o_send, o_recv, peer).start()

    def sent(b, carry):
        copy1(b).wait_send()
        all2(b).wait_send()
        all3(b).wait_send()
        copy4(b).wait_send()
        return carry

    lax.fori_loop(0, steps, sent, 0)
    for i in range(2):
        along_pts(rows_in, rows_in, c_send.at[i], c_recv.at[i], here).wait_send()
    along_pts(prod_in, prod_in, o_send, o_recv, here).wait_recv()
    total = prod_t[here]
    for k in range(GROUPS - 1):
        total = total + prod_in[k]
    out[...] = total
    along_pts(prod_in, prod_in, o_send, o_recv, here).wait_send()


def per_device(points, landmark_ids, coefficients):
    pts_rows, width = points.shape
    marks, outs = coefficients.shape
    steps = pts_rows // STEP
    vmem = pl.BlockSpec(memory_space=pltpu.VMEM)
    dma = pltpu.SemaphoreType.DMA
    product = pl.pallas_call(
        functools.partial(body, steps),
        out_shape=jax.ShapeDtypeStruct((outs, marks // GROUPS), F32),
        in_specs=[pl.BlockSpec(memory_space=pltpu.SMEM), vmem, pl.BlockSpec(memory_space=pl.ANY)],
        out_specs=vmem,
        scratch_shapes=[
            pltpu.VMEM((pts_rows, width), BF16),
            pltpu.VMEM((steps, PIECES, TILE), F32),
            pltpu.VMEM((marks, width + 128), BF16),
            pltpu.VMEM((marks // GROUPS, width), F32),
            pltpu.VMEM((GROUPS, marks // GROUPS, width), BF16),
            pltpu.VMEM((GROUPS - 1, marks // GROUPS, width), BF16),
            pltpu.VMEM((GROUPS, marks // GROUPS, width), BF16),
            pltpu.VMEM((2, marks, TILE), BF16),
            pltpu.VMEM((2, marks, TILE), BF16),
            pltpu.VMEM((2 + steps * PIECES, outs, TILE), BF16),
            pltpu.VMEM((steps, GROUPS, outs, TILE), BF16),
            pltpu.VMEM((steps, GROUPS, outs, TILE), BF16),
            pltpu.VMEM((steps, GROUPS - 1, outs, TILE), BF16),
            pltpu.VMEM((BLANK + steps * PIECES, outs, TILE), BF16),
            pltpu.VMEM((GROUPS, outs, 128), F32),
            pltpu.VMEM((GROUPS - 1, outs, 128), F32),
            dma((steps,)),
            dma((2,)),
            dma((2,)),
        ]
        + [dma((steps,))] * 8
        + [dma(()), dma(())],
        compiler_params=pltpu.CompilerParams(collective_id=0, has_side_effects=True, vmem_limit_bytes=60 * 2**20),
    )(landmark_ids, coefficients.T, points)
    return product.T / (pts_rows * GROUPS)


def solution(mesh):
    placed = (P("pts", None), P("lmk"), P("lmk", None))
    with jax.sharding.use_abstract_mesh(mesh.abstract_mesh):
        return jax.shard_map(
            per_device, mesh=mesh, in_specs=placed, out_specs=P(("lmk", "pts"), None), check_vma=False
        )
```

```python
import functools

import jax
import jax.numpy as jnp
from jax import lax
from jax.experimental import pallas as pl
from jax.experimental.pallas import tpu as pltpu
from jax.sharding import PartitionSpec as P

MESH = pl.DeviceIdType.MESH
BF16, F32 = jnp.bfloat16, jnp.float32
GROUPS = 8
TILE = 256
UNITS = 8
PIECES = 2 * UNITS
STEP = PIECES * TILE
HALF = UNITS // 2
LAG = 8
BACK = LAG * HALF + 3
KEPT = (BACK + 1) // 2
BLANK = 2 * (BACK - LAG * HALF)
SEG, RING = 64, 7
MXUS = (0, 1)


def augment(rows_f):
    sq = -0.25 * jnp.sum(rows_f * rows_f, axis=1, keepdims=True)
    hi = sq.astype(BF16).astype(F32)
    mid = (sq - hi).astype(BF16).astype(F32)
    low = sq - hi - mid
    lane = lax.broadcasted_iota(jnp.int32, rows_f.shape, 1)
    return jnp.where(lane == 0, hi, jnp.where(lane == 1, mid, jnp.where(lane == 2, low, 0.0))).astype(BF16)


def halves(rows):
    rows_f = rows.astype(F32)
    squares = rows_f * rows_f
    hi = squares.astype(BF16)
    return jnp.concatenate([hi, (squares - hi.astype(F32)).astype(BF16)], axis=1)


def body(steps, ids, ct, points, out, xm, sq, ca, picked_f, picked, rows_in, centers, pb0, pb1, part, p1r, p2s, p2r,
         fit, prod_t, prod_in, load_sem, c_send, c_recv, s1, r1, s2, r2, s3, r3, s4, r4, o_send, o_recv):
    here = lax.axis_index("pts")
    lmk = lax.axis_index("lmk")
    chip, core = lmk // 2, lmk % 2
    other = chip * 2 + 1 - core
    slab, width = xm.shape
    outs, marks = ct.shape
    pb = (pb0, pb1)

    def load(i):
        rows = pl.ds(i * STEP, STEP)
        return pltpu.make_async_copy(points.at[rows], xm.at[rows], load_sem.at[i])

    def start_load(i, carry):
        load(i).start()
        return carry

    lax.fori_loop(0, steps, start_load, 0)

    barrier = pltpu.get_barrier_semaphore()
    for k in range(GROUPS - 1):
        pl.semaphore_signal(barrier, inc=1, device_id={"pts": (here + k + 1) % GROUPS}, device_id_type=MESH)
        pl.semaphore_signal(barrier, inc=1, device_id={"lmk": ((chip + k + 1) % GROUPS) * 2 + core}, device_id_type=MESH)
    pl.semaphore_signal(barrier, inc=1, device_id={"lmk": other}, device_id_type=MESH)

    def along_pts(src, dst, send, recv, peer):
        return pltpu.make_async_remote_copy(src, dst, send, recv, device_id={"pts": peer}, device_id_type=MESH)

    def along_lmk(src, dst, send, recv, peer):
        return pltpu.make_async_remote_copy(src, dst, send, recv, device_id={"lmk": peer}, device_id_type=MESH)

    def gather(xf):
        def widen(i, carry):
            load(i).wait()
            for h in range(8):
                rows = pl.ds(i * STEP + h * (STEP // 8), STEP // 8)
                xf[rows, :] = xm[rows, :].astype(F32)
            return carry

        lax.fori_loop(0, steps, widen, 0)

        def pick(k, carry):
            peer = (here + k + 1) % GROUPS

            def some(i, carry):
                for u in range(32):
                    row_at = i * 32 + u
                    at = ids[peer * 128 + row_at] - here * slab
                    row = xf[pl.ds(jnp.clip(at, 0, slab - 1), 1), :]
                    picked_f[pl.ds(row_at, 1), :] = jnp.where((at >= 0) & (at < slab), row, 0.0)
                return carry

            lax.fori_loop(0, 4, some, 0)
            picked[peer] = picked_f[...].astype(BF16)

            @pl.when(k < GROUPS - 1)
            def _():
                along_pts(picked.at[peer], rows_in.at[k], c_send.at[0], c_recv.at[0], peer).start()

            return carry

        pl.semaphore_wait(barrier, 2 * GROUPS - 1)
        lax.fori_loop(0, GROUPS, pick, 0)

    pl.run_scoped(gather, pltpu.VMEM((slab, width), F32))

    def norms_of(low, high):
        def scoped(accs):
            quarter = jnp.full((32, TILE), -0.25, BF16)

            def some(i, carry):
                for h in range(0, PIECES, 4):
                    for q in range(h, h + 4):
                        rows = halves(xm[pl.ds(i * STEP + q * TILE, TILE), :])
                        pltpu.matmul_push_rhs(rows, q // 2 % 2, q % 2, transpose=True)
                        pltpu.matmul_acc_lhs(accs[q % 4], quarter, q // 2 % 2)
                    for q in range(h, h + 4):
                        sq[i, pl.ds(q, 1), :] = pltpu.matmul_pop(accs[q % 4])[:1]
                return carry

            lax.fori_loop(low, high, some, 0)

        pl.run_scoped(scoped, [pltpu.ACC(q % 2)((32, TILE), F32) for q in range(4)])

    norms_of(0, steps // 2)
    along_pts(rows_in, rows_in, c_send.at[0], c_recv.at[0], here).wait_recv()
    total = picked[here].astype(F32)
    for k in range(GROUPS - 1):
        total = total + rows_in[k].astype(F32)
    centers[here] = total.astype(BF16)
    for k in range(GROUPS - 1):
        peer = (here + k + 1) % GROUPS
        along_pts(centers.at[here], centers.at[here], c_send.at[1], c_recv.at[1], peer).start()
    norms_of(steps // 2, steps)
    pb1[...] = jnp.zeros_like(pb1)
    along_pts(rows_in, rows_in, c_send.at[1], c_recv.at[1], here).wait_recv()
    for g in range(GROUPS):
        rows_f = centers[g].astype(F32)
        ca[pl.ds(g * 128, 128), pl.ds(0, 128)] = (0.5 * rows_f).astype(BF16)
        ca[pl.ds(g * 128, 128), pl.ds(128, 128)] = augment(rows_f)

    def copy1(b):
        mine = part.at[pl.ds(2 + b * PIECES + (1 - core) * GROUPS, GROUPS)]
        return along_lmk(mine, p1r.at[b], s1.at[b], r1.at[b], other)

    def copy4(b):
        half = fit.at[pl.ds(BLANK + b * PIECES + core * GROUPS, GROUPS)]
        return along_lmk(half, half, s4.at[b], r4.at[b], other)

    def all2(b):
        return along_lmk(p2r.at[b], p2r.at[b], s2.at[b], r2.at[b], other)

    def all3(b):
        return along_lmk(p2r.at[b], p2r.at[b], s3.at[b], r3.at[b], other)

    def send1(b):
        copy1(b).start()

    def send2(b):
        copy1(b).wait_recv()
        for g in range(GROUPS):
            own = part[2 + b * PIECES + core * GROUPS + g]
            p2s[b, g] = (own.astype(F32) + p1r[b, g].astype(F32)).astype(BF16)
        for k in range(GROUPS - 1):
            peer = (chip + k + 1) % GROUPS
            along_lmk(p2s.at[b, peer], p2r.at[b, k], s2.at[b], r2.at[b], peer * 2 + core).start()

    def send3(b):
        all2(b).wait_recv()
        total = p2s[b, chip].astype(F32)
        for k in range(GROUPS - 1):
            total = total + p2r[b, k].astype(F32)
        mine = BLANK + b * PIECES + core * GROUPS + chip
        fit[mine] = total.astype(BF16)
        for k in range(GROUPS - 1):
            peer = (chip + k + 1) % GROUPS
            along_lmk(fit.at[mine], fit.at[mine], s3.at[b], r3.at[b], peer * 2 + core).start()

    def send4(b):
        all3(b).wait_recv()
        copy4(b).start()

    lane = lax.broadcasted_iota(jnp.int32, (TILE, 128), 1)
    ones = jnp.where(lane < 3, 1.0, 0.0).astype(BF16)
    blank = jnp.zeros((TILE - outs, TILE), BF16)
    segs = marks // SEG

    def main(accs, kts):
        def push_points(unit, m, reg):
            at = pl.multiple_of((unit * 2 + m) * TILE, TILE)
            rows = jnp.concatenate([xm[pl.ds(at, TILE), :], ones], axis=1)
            pltpu.matmul_push_rhs(rows, reg, m, transpose=True)

        def push_tile(par, m, q, reg):
            pltpu.matmul_push_rhs(pb[par][m, pl.ds(q * TILE, TILE), :], reg, m)

        def push_fitted(unit, c, m, reg):
            pltpu.matmul_push_rhs(jnp.concatenate([fit[BLANK + unit * 2 + c], blank], axis=0), reg, m, transpose=True)

        def first_product(unit, par, m, q, reg):
            acc = accs[m]["B"]
            pltpu.matmul_acc_lhs(acc, ct[:, pl.ds(q * TILE, TILE)], reg)
            if q == 3:
                part[unit * 2 + m] = pltpu.matmul_pop(acc).astype(BF16)

        def second_product(unit, par, c, m, reg):
            tile = kts[par][lax.rem(unit // 2 + KEPT, KEPT), c, pl.ds(m * (marks // 2), marks // 2), :]
            pltpu.matmul_acc_lhs(accs[m]["C"], tile, reg)

        def unit_step(h, i, par, second):
            unit = h * HALF + i
            slot = lax.rem(unit // 2, KEPT)
            after = jnp.minimum(unit + 1, steps * UNITS - 1)
            norms = [sq[unit // UNITS, pl.ds((unit % UNITS) * 2 + m, 1), :] for m in MXUS]

            def finish(m, s):
                tile = jnp.exp(pltpu.matmul_pop(accs[m]["A"][s % RING]) + norms[m]).astype(BF16)
                rows = pl.ds(s * SEG, SEG)
                kts[par][slot, m, rows, :] = tile
                pb[par][m, rows, :] = tile

            def distances(m, low, high):
                for s in range(low, high):
                    if s >= RING:
                        finish(m, s - RING)
                    acc = accs[m]["A"][s % RING]
                    pltpu.matmul_acc_lhs(acc, ca[pl.ds(s * SEG, SEG), :], 0 if s == low else None)

            def tail():
                for s in range(segs - RING, segs):
                    for m in MXUS:
                        finish(m, s)

            def each(f, *args):
                for m in MXUS:
                    f(*(m if a is MXUS else a for a in args))

            each(distances, MXUS, 0, segs // 2 if second else 3 * segs // 8)
            if second:
                before = unit - BACK
                each(push_fitted, before, 0, MXUS, 0)
                each(first_product, unit, par, MXUS, 0, 1)
                each(push_tile, 1 - par, MXUS, 1, 1)
                each(second_product, before, 1 - par, 0, MXUS, 0)
                each(push_points, unit, MXUS, 0)
                each(first_product, unit, par, MXUS, 1, 1)
                each(push_tile, 1 - par, MXUS, 2, 1)
                each(distances, MXUS, segs // 2, segs)
                each(push_fitted, before, 1, MXUS, 0)
                each(first_product, unit, par, MXUS, 2, 1)
                each(push_tile, 1 - par, MXUS, 3, 1)
                each(second_product, before, 1 - par, 1, MXUS, 0)
                tail()
                each(push_points, after, MXUS, 0)
                each(first_product, unit, par, MXUS, 3, 1)
                each(push_tile, par, MXUS, 0, 1)
            else:
                each(push_points, unit, MXUS, 0)
                each(first_product, unit, par, MXUS, 0, 1)
                each(push_tile, 1 - par, MXUS, 1, 1)
                each(distances, MXUS, 3 * segs // 8, 3 * segs // 4)
                each(push_points, unit, MXUS, 0)
                each(first_product, unit, par, MXUS, 1, 1)
                each(push_tile, 1 - par, MXUS, 2, 1)
                each(distances, MXUS, 3 * segs // 4, segs)
                each(push_tile, 1 - par, MXUS, 3, 0)
                each(first_product, unit, par, MXUS, 2, 1)
                tail()
                each(push_tile, par, MXUS, 0, 1)
                each(first_product, unit, par, MXUS, 3, 0)
                each(push_points, after, MXUS, 0)

        for m in MXUS:
            push_points(0, m, 0)
            push_tile(1, m, 0, 1)

        def exchange(h):
            for stage, behind in ((send2, 3), (send3, 5), (send4, 7)):
                due = (h % 2 == 1) & (h >= behind) & (h < behind + 2 * steps)
                pl.when(due)(functools.partial(stage, (h - behind) // 2))

        def tiles(low, high, second):
            def half(h, carry):
                def pair(i, carry):
                    @pl.when(i == 1)
                    def _():
                        pl.when((h % 2 == 0) & (h >= 2))(functools.partial(send1, h // 2 - 1))
                        exchange(h)
                        if second:
                            pl.when(h % 2 == 0)(lambda: copy4((h - LAG) // 2).wait_recv())

                    unit_step(h, i * 2, 0, second)
                    unit_step(h, i * 2 + 1, 1, second)
                    return carry

                return lax.fori_loop(0, HALF // 2, pair, carry)

            lax.fori_loop(low, high, half, 0)

        for unit in range(LAG * HALF - BACK, 0):
            kts[unit % 2][unit // 2 + KEPT] = jnp.zeros((2, marks, TILE), BF16)
        fit[pl.ds(0, BLANK)] = jnp.zeros((BLANK, outs, TILE), BF16)
        tiles(0, LAG, False)
        tiles(LAG, 2 * steps, True)

        def second_only(first, count):
            turns = [(first + i, (count + i) % 2, c) for i in range(count) for c in range(2)]
            for unit, _, c in turns[:2]:
                for m in MXUS:
                    push_fitted(unit, c, m, c)
            for at, (unit, par, c) in enumerate(turns):
                for m in MXUS:
                    second_product(unit, par, c, m, c)
                    if at + 2 < len(turns):
                        push_fitted(turns[at + 2][0], c, m, c)

        last = steps * UNITS
        for m in MXUS:
            pltpu.matmul_acc_lhs(accs[m]["A"][0], ca[pl.ds(0, SEG), :], 0)
            push_tile(1, m, 1, 0)
            first_product(last, 0, m, 0, 1)
            push_tile(1, m, 2, 1)
            first_product(last, 0, m, 1, 0)
            push_tile(1, m, 3, 0)
            first_product(last, 0, m, 2, 1)
            first_product(last, 0, m, 3, 0)
            pltpu.matmul_pop(accs[m]["A"][0])

        def rest(h, carry):
            exchange(h + 1)
            pl.when(h % 2 == 0)(lambda: copy4((h - LAG) // 2).wait_recv())
            second_only((h - LAG) * HALF, HALF)
            return carry

        send1(steps - 1)
        ahead = BACK - LAG * HALF
        second_only((2 * steps - LAG) * HALF - ahead, ahead)
        lax.fori_loop(2 * steps, 2 * steps + LAG, rest, 0)

        for m in MXUS:
            total = pltpu.matmul_pop(accs[m]["C"])
            for g in range(GROUPS // 2):
                prod_t[m * (GROUPS // 2) + g] = total[g * 128 : (g + 1) * 128, :128].T[:outs]

    def acc(m):
        of = pltpu.ACC(m)
        return {"A": [of((SEG, TILE), F32)] * RING, "B": of((outs, TILE), F32), "C": of((marks // 2, TILE), F32)}

    pl.run_scoped(main, [acc(m) for m in MXUS], [pltpu.VMEM((KEPT, 2, marks, TILE), BF16)] * 2)

    for k in range(GROUPS - 1):
        peer = (here + k + 1) % GROUPS
        along_pts(prod_t.at[peer], prod_in.at[k], o_send, o_recv, peer).start()

    def sent(b, carry):
        copy1(b).wait_send()
        all2(b).wait_send()
        all3(b).wait_send()
        copy4(b).wait_send()
        return carry

    lax.fori_loop(0, steps, sent, 0)
    for i in range(2):
        along_pts(rows_in, rows_in, c_send.at[i], c_recv.at[i], here).wait_send()
    along_pts(prod_in, prod_in, o_send, o_recv, here).wait_recv()
    total = prod_t[here]
    for k in range(GROUPS - 1):
        total = total + prod_in[k]
    out[...] = total
    along_pts(prod_in, prod_in, o_send, o_recv, here).wait_send()


def per_device(points, landmark_ids, coefficients):
    pts_rows, width = points.shape
    marks, outs = coefficients.shape
    steps = pts_rows // STEP
    vmem = pl.BlockSpec(memory_space=pltpu.VMEM)
    dma = pltpu.SemaphoreType.DMA
    product = pl.pallas_call(
        functools.partial(body, steps),
        out_shape=jax.ShapeDtypeStruct((outs, marks // GROUPS), F32),
        in_specs=[pl.BlockSpec(memory_space=pltpu.SMEM), vmem, pl.BlockSpec(memory_space=pl.ANY)],
        out_specs=vmem,
        scratch_shapes=[
            pltpu.VMEM((pts_rows, width), BF16),
            pltpu.VMEM((steps, PIECES, TILE), F32),
            pltpu.VMEM((marks, width + 128), BF16),
            pltpu.VMEM((marks // GROUPS, width), F32),
            pltpu.VMEM((GROUPS, marks // GROUPS, width), BF16),
            pltpu.VMEM((GROUPS - 1, marks // GROUPS, width), BF16),
            pltpu.VMEM((GROUPS, marks // GROUPS, width), BF16),
            pltpu.VMEM((2, marks, TILE), BF16),
            pltpu.VMEM((2, marks, TILE), BF16),
            pltpu.VMEM((2 + steps * PIECES, outs, TILE), BF16),
            pltpu.VMEM((steps, GROUPS, outs, TILE), BF16),
            pltpu.VMEM((steps, GROUPS, outs, TILE), BF16),
            pltpu.VMEM((steps, GROUPS - 1, outs, TILE), BF16),
            pltpu.VMEM((BLANK + steps * PIECES, outs, TILE), BF16),
            pltpu.VMEM((GROUPS, outs, 128), F32),
            pltpu.VMEM((GROUPS - 1, outs, 128), F32),
            dma((steps,)),
            dma((2,)),
            dma((2,)),
        ]
        + [dma((steps,))] * 8
        + [dma(()), dma(())],
        compiler_params=pltpu.CompilerParams(collective_id=0, has_side_effects=True, vmem_limit_bytes=60 * 2**20),
    )(landmark_ids, coefficients.T, points)
    return product.T / (pts_rows * GROUPS)


def solution(mesh):
    placed = (P("pts", None), P("lmk"), P("lmk", None))
    with jax.sharding.use_abstract_mesh(mesh.abstract_mesh):
        return jax.shard_map(
            per_device, mesh=mesh, in_specs=placed, out_specs=P(("lmk", "pts"), None), check_vma=False
        )
```

```python
import functools

import jax
import jax.numpy as jnp
from jax import lax
from jax.experimental import pallas as pl
from jax.experimental.pallas import tpu as pltpu
from jax.sharding import PartitionSpec as P

MESH = pl.DeviceIdType.MESH
BF16, F32 = jnp.bfloat16, jnp.float32
GROUPS = 8
TILE = 256
UNITS = 8
PIECES = 2 * UNITS
STEP = PIECES * TILE
HALF = UNITS // 2
LAG = 8
BACK = LAG * HALF + 3
KEPT = (BACK + 1) // 2
BLANK = 2 * (BACK - LAG * HALF)
SEG, RING = 64, 7
MXUS = (0, 1)


def augment(rows_f):
    sq = -0.25 * jnp.sum(rows_f * rows_f, axis=1, keepdims=True)
    hi = sq.astype(BF16).astype(F32)
    mid = (sq - hi).astype(BF16).astype(F32)
    low = sq - hi - mid
    lane = lax.broadcasted_iota(jnp.int32, rows_f.shape, 1)
    return jnp.where(lane == 0, hi, jnp.where(lane == 1, mid, jnp.where(lane == 2, low, 0.0))).astype(BF16)


def halves(rows):
    rows_f = rows.astype(F32)
    squares = rows_f * rows_f
    hi = squares.astype(BF16)
    return jnp.concatenate([hi, (squares - hi.astype(F32)).astype(BF16)], axis=1)


def body(steps, ids, ct, points, out, xm, sq, ca, picked_f, picked, rows_in, centers, pb0, pb1, part, p1r, p2s, p2r,
         fit, end_in, prod_t, prod_in, load_sem, c_send, c_recv, s1, r1, s2, r2, s3, r3, s4, r4, e1, e2, e3, e4, o_send, o_recv):
    here = lax.axis_index("pts")
    lmk = lax.axis_index("lmk")
    chip, core = lmk // 2, lmk % 2
    other = chip * 2 + 1 - core
    slab, width = xm.shape
    outs, marks = ct.shape
    pb = (pb0, pb1)

    def load(i):
        rows = pl.ds(i * STEP, STEP)
        return pltpu.make_async_copy(points.at[rows], xm.at[rows], load_sem.at[i])

    def start_load(i, carry):
        load(i).start()
        return carry

    lax.fori_loop(0, steps, start_load, 0)

    barrier = pltpu.get_barrier_semaphore()
    for k in range(GROUPS - 1):
        pl.semaphore_signal(barrier, inc=1, device_id={"pts": (here + k + 1) % GROUPS}, device_id_type=MESH)
        pl.semaphore_signal(barrier, inc=1, device_id={"lmk": ((chip + k + 1) % GROUPS) * 2 + core}, device_id_type=MESH)
    pl.semaphore_signal(barrier, inc=1, device_id={"lmk": other}, device_id_type=MESH)

    def along_pts(src, dst, send, recv, peer):
        return pltpu.make_async_remote_copy(src, dst, send, recv, device_id={"pts": peer}, device_id_type=MESH)

    def along_lmk(src, dst, send, recv, peer):
        return pltpu.make_async_remote_copy(src, dst, send, recv, device_id={"lmk": peer}, device_id_type=MESH)

    def gather(xf):
        def widen(i, carry):
            load(i).wait()
            for h in range(8):
                rows = pl.ds(i * STEP + h * (STEP // 8), STEP // 8)
                xf[rows, :] = xm[rows, :].astype(F32)
            return carry

        lax.fori_loop(0, steps, widen, 0)

        def pick(k, carry):
            peer = (here + k + 1) % GROUPS

            def some(i, carry):
                for u in range(32):
                    row_at = i * 32 + u
                    at = ids[peer * 128 + row_at] - here * slab
                    row = xf[pl.ds(jnp.clip(at, 0, slab - 1), 1), :]
                    picked_f[pl.ds(row_at, 1), :] = jnp.where((at >= 0) & (at < slab), row, 0.0)
                return carry

            lax.fori_loop(0, 4, some, 0)
            picked[peer] = picked_f[...].astype(BF16)

            @pl.when(k < GROUPS - 1)
            def _():
                along_pts(picked.at[peer], rows_in.at[k], c_send.at[0], c_recv.at[0], peer).start()

            return carry

        pl.semaphore_wait(barrier, 2 * GROUPS - 1)
        lax.fori_loop(0, GROUPS, pick, 0)

    pl.run_scoped(gather, pltpu.VMEM((slab, width), F32))

    def norms_of(low, high):
        def scoped(accs):
            quarter = jnp.full((32, TILE), -0.25, BF16)

            def some(i, carry):
                for h in range(0, PIECES, 4):
                    for q in range(h, h + 4):
                        rows = halves(xm[pl.ds(i * STEP + q * TILE, TILE), :])
                        pltpu.matmul_push_rhs(rows, q // 2 % 2, q % 2, transpose=True)
                        pltpu.matmul_acc_lhs(accs[q % 4], quarter, q // 2 % 2)
                    for q in range(h, h + 4):
                        sq[i, pl.ds(q, 1), :] = pltpu.matmul_pop(accs[q % 4])[:1]
                return carry

            lax.fori_loop(low, high, some, 0)

        pl.run_scoped(scoped, [pltpu.ACC(q % 2)((32, TILE), F32) for q in range(4)])

    norms_of(0, steps // 2)
    along_pts(rows_in, rows_in, c_send.at[0], c_recv.at[0], here).wait_recv()
    total = picked[here].astype(F32)
    for k in range(GROUPS - 1):
        total = total + rows_in[k].astype(F32)
    centers[here] = total.astype(BF16)
    for k in range(GROUPS - 1):
        peer = (here + k + 1) % GROUPS
        along_pts(centers.at[here], centers.at[here], c_send.at[1], c_recv.at[1], peer).start()
    norms_of(steps // 2, steps)
    pb1[...] = jnp.zeros_like(pb1)
    along_pts(rows_in, rows_in, c_send.at[1], c_recv.at[1], here).wait_recv()
    for g in range(GROUPS):
        rows_f = centers[g].astype(F32)
        ca[pl.ds(g * 128, 128), pl.ds(0, 128)] = (0.5 * rows_f).astype(BF16)
        ca[pl.ds(g * 128, 128), pl.ds(128, 128)] = augment(rows_f)

    def copy1(b):
        mine = part.at[pl.ds(2 + b * PIECES + (1 - core) * GROUPS, GROUPS)]
        return along_lmk(mine, p1r.at[b], s1.at[b], r1.at[b], other)

    def copy4(b):
        half = fit.at[pl.ds(BLANK + b * PIECES + core * GROUPS, GROUPS)]
        return along_lmk(half, half, s4.at[b], r4.at[b], other)

    def all2(b):
        return along_lmk(p2r.at[b], p2r.at[b], s2.at[b], r2.at[b], other)

    def all3(b):
        return along_lmk(p2r.at[b], p2r.at[b], s3.at[b], r3.at[b], other)

    def send1(b):
        copy1(b).start()

    def send2(b):
        copy1(b).wait_recv()
        for g in range(GROUPS):
            own = part[2 + b * PIECES + core * GROUPS + g]
            p2s[b, g] = (own.astype(F32) + p1r[b, g].astype(F32)).astype(BF16)
        for k in range(GROUPS - 1):
            peer = (chip + k + 1) % GROUPS
            along_lmk(p2s.at[b, peer], p2r.at[b, k], s2.at[b], r2.at[b], peer * 2 + core).start()

    def send3(b):
        all2(b).wait_recv()
        total = p2s[b, chip].astype(F32)
        for k in range(GROUPS - 1):
            total = total + p2r[b, k].astype(F32)
        mine = BLANK + b * PIECES + core * GROUPS + chip
        fit[mine] = total.astype(BF16)
        for k in range(GROUPS - 1):
            peer = (chip + k + 1) % GROUPS
            along_lmk(fit.at[mine], fit.at[mine], s3.at[b], r3.at[b], peer * 2 + core).start()

    def send4(b):
        all3(b).wait_recv()
        copy4(b).start()

    lane = lax.broadcasted_iota(jnp.int32, (TILE, 128), 1)
    ones = jnp.where(lane < 3, 1.0, 0.0).astype(BF16)
    blank = jnp.zeros((TILE - outs, TILE), BF16)
    segs = marks // SEG

    def main(accs, kts):
        def push_points(unit, m, reg):
            at = pl.multiple_of((unit * 2 + m) * TILE, TILE)
            rows = jnp.concatenate([xm[pl.ds(at, TILE), :], ones], axis=1)
            pltpu.matmul_push_rhs(rows, reg, m, transpose=True)

        def push_tile(par, m, q, reg):
            pltpu.matmul_push_rhs(pb[par][m, pl.ds(q * TILE, TILE), :], reg, m)

        def push_fitted(unit, c, m, reg):
            pltpu.matmul_push_rhs(jnp.concatenate([fit[BLANK + unit * 2 + c], blank], axis=0), reg, m, transpose=True)

        def first_product(unit, par, m, q, reg):
            acc = accs[m]["B"]
            pltpu.matmul_acc_lhs(acc, ct[:, pl.ds(q * TILE, TILE)], reg)
            if q == 3:
                part[unit * 2 + m] = pltpu.matmul_pop(acc).astype(BF16)

        def second_product(unit, par, c, m, reg):
            tile = kts[par][lax.rem(unit // 2 + KEPT, KEPT), c, pl.ds(m * (marks // 2), marks // 2), :]
            pltpu.matmul_acc_lhs(accs[m]["C"], tile, reg)

        def unit_step(h, i, par, second):
            unit = h * HALF + i
            slot = lax.rem(unit // 2, KEPT)
            after = jnp.minimum(unit + 1, steps * UNITS - 1)
            norms = [sq[unit // UNITS, pl.ds((unit % UNITS) * 2 + m, 1), :] for m in MXUS]

            def finish(m, s):
                tile = jnp.exp(pltpu.matmul_pop(accs[m]["A"][s % RING]) + norms[m]).astype(BF16)
                rows = pl.ds(s * SEG, SEG)
                kts[par][slot, m, rows, :] = tile
                pb[par][m, rows, :] = tile

            def distances(m, low, high):
                for s in range(low, high):
                    if s >= RING:
                        finish(m, s - RING)
                    acc = accs[m]["A"][s % RING]
                    pltpu.matmul_acc_lhs(acc, ca[pl.ds(s * SEG, SEG), :], 0 if s == low else None)

            def tail():
                for s in range(segs - RING, segs):
                    for m in MXUS:
                        finish(m, s)

            def each(f, *args):
                for m in MXUS:
                    f(*(m if a is MXUS else a for a in args))

            each(distances, MXUS, 0, segs // 2 if second else 3 * segs // 8)
            if second:
                before = unit - BACK
                each(push_fitted, before, 0, MXUS, 0)
                each(first_product, unit, par, MXUS, 0, 1)
                each(push_tile, 1 - par, MXUS, 1, 1)
                each(second_product, before, 1 - par, 0, MXUS, 0)
                each(push_points, unit, MXUS, 0)
                each(first_product, unit, par, MXUS, 1, 1)
                each(push_tile, 1 - par, MXUS, 2, 1)
                each(distances, MXUS, segs // 2, segs)
                each(push_fitted, before, 1, MXUS, 0)
                each(first_product, unit, par, MXUS, 2, 1)
                each(push_tile, 1 - par, MXUS, 3, 1)
                each(second_product, before, 1 - par, 1, MXUS, 0)
                tail()
                each(push_points, after, MXUS, 0)
                each(first_product, unit, par, MXUS, 3, 1)
                each(push_tile, par, MXUS, 0, 1)
            else:
                each(push_points, unit, MXUS, 0)
                each(first_product, unit, par, MXUS, 0, 1)
                each(push_tile, 1 - par, MXUS, 1, 1)
                each(distances, MXUS, 3 * segs // 8, 3 * segs // 4)
                each(push_points, unit, MXUS, 0)
                each(first_product, unit, par, MXUS, 1, 1)
                each(push_tile, 1 - par, MXUS, 2, 1)
                each(distances, MXUS, 3 * segs // 4, segs)
                each(push_tile, 1 - par, MXUS, 3, 0)
                each(first_product, unit, par, MXUS, 2, 1)
                tail()
                each(push_tile, par, MXUS, 0, 1)
                each(first_product, unit, par, MXUS, 3, 0)
                each(push_points, after, MXUS, 0)

        for m in MXUS:
            push_points(0, m, 0)
            push_tile(1, m, 0, 1)

        def exchange(h):
            for stage, behind in ((send2, 3), (send3, 5), (send4, 7)):
                due = (h % 2 == 1) & (h >= behind)
                pl.when(due)(functools.partial(stage, (h - behind) // 2))

        end = steps - 1
        lanes = pl.ds(pl.multiple_of(chip % 2 * 128, 128), 128)
        share = GROUPS // 2

        def end1(e):
            mine = part.at[pl.ds(2 + end * PIECES + e * GROUPS + (1 - core) * share, share)]
            return along_lmk(mine, p1r.at[end, pl.ds(e * share, share)], e1.at[0, e], e1.at[1, e], other)

        def all_end(stage, e):
            return along_lmk(end_in.at[e], end_in.at[e], stage.at[0, e], stage.at[1, e], other)

        def end4(e):
            half = fit.at[pl.ds(BLANK + end * PIECES + e * GROUPS + core * share, share)]
            return along_lmk(half, half, e4.at[0, e], e4.at[1, e], other)

        def end_send2(e):
            end1(e).wait_recv()
            for g in range(share):
                own = part[2 + end * PIECES + e * GROUPS + core * share + g]
                p2s[end, e * share + g] = (own.astype(F32) + p1r[end, e * share + g].astype(F32)).astype(BF16)
            for k in range(GROUPS - 1):
                peer = (chip + k + 1) % GROUPS
                theirs = pl.ds(pl.multiple_of(peer % 2 * 128, 128), 128)
                src = p2s.at[end, e * share + peer // 2, :, theirs]
                along_lmk(src, end_in.at[e, k], e2.at[0, e], e2.at[1, e], peer * 2 + core).start()

        def end_send3(e):
            all_end(e2, e).wait_recv()
            total = p2s[end, e * share + chip // 2, :, lanes].astype(F32)
            for k in range(GROUPS - 1):
                total = total + end_in[e, k].astype(F32)
            mine = BLANK + end * PIECES + e * GROUPS + core * share + chip // 2
            fit[mine, :, lanes] = total.astype(BF16)
            for k in range(GROUPS - 1):
                peer = (chip + k + 1) % GROUPS
                piece = fit.at[mine, :, lanes]
                along_lmk(piece, piece, e3.at[0, e], e3.at[1, e], peer * 2 + core).start()

        def end_send4(e):
            all_end(e3, e).wait_recv()
            end4(e).start()

        def tiles(low, high, second):
            def half(h, carry):
                def pair(i, carry):
                    @pl.when(((i == 1) & (h < 2 * steps - 1)) | ((i == 0) & (h == 2 * steps - 1)))
                    def _():
                        pl.when((h % 2 == 0) & (h >= 2))(functools.partial(send1, h // 2 - 1))
                        exchange(h)
                        if second:
                            pl.when(h % 2 == 0)(lambda: copy4((h - LAG) // 2).wait_recv())

                    if second:
                        pl.when((i == 1) & (h == 2 * steps - 1))(lambda: end1(0).start())
                    unit_step(h, i * 2, 0, second)
                    unit_step(h, i * 2 + 1, 1, second)
                    return carry

                return lax.fori_loop(0, HALF // 2, pair, carry)

            lax.fori_loop(low, high, half, 0)

        for unit in range(LAG * HALF - BACK, 0):
            kts[unit % 2][unit // 2 + KEPT] = jnp.zeros((2, marks, TILE), BF16)
        fit[pl.ds(0, BLANK)] = jnp.zeros((BLANK, outs, TILE), BF16)
        tiles(0, LAG, False)
        tiles(LAG, 2 * steps, True)

        def second_only(first, count):
            turns = [(first + i, (count + i) % 2, c) for i in range(count) for c in range(2)]
            for unit, _, c in turns[:2]:
                for m in MXUS:
                    push_fitted(unit, c, m, c)
            for at, (unit, par, c) in enumerate(turns):
                for m in MXUS:
                    second_product(unit, par, c, m, c)
                    if at + 2 < len(turns):
                        push_fitted(turns[at + 2][0], c, m, c)

        last = steps * UNITS
        for m in MXUS:
            pltpu.matmul_acc_lhs(accs[m]["A"][0], ca[pl.ds(0, SEG), :], 0)
            push_tile(1, m, 1, 0)
            first_product(last, 0, m, 0, 1)
            push_tile(1, m, 2, 1)
            first_product(last, 0, m, 1, 0)
            push_tile(1, m, 3, 0)
            first_product(last, 0, m, 2, 1)
            first_product(last, 0, m, 3, 0)
            pltpu.matmul_pop(accs[m]["A"][0])

        end1(1).start()
        end_send2(0)
        ahead = BACK - LAG * HALF
        second_only((2 * steps - LAG) * HALF - ahead, ahead)
        end_send2(1)
        copy4(end - 3).wait_recv()
        second_only((2 * steps - LAG) * HALF, HALF)
        send3(end - 1)
        send4(end - 2)
        second_only((2 * steps - LAG + 1) * HALF, HALF)
        copy4(end - 2).wait_recv()
        second_only((2 * steps - LAG + 2) * HALF, HALF)
        end_send3(0)
        end_send3(1)
        second_only((2 * steps - LAG + 3) * HALF, HALF)
        send4(end - 1)
        copy4(end - 1).wait_recv()
        second_only((2 * steps - LAG + 4) * HALF, HALF)
        end_send4(0)
        second_only((2 * steps - LAG + 5) * HALF, HALF)
        end_send4(1)
        end4(0).wait_recv()
        second_only((2 * steps - LAG + 6) * HALF, HALF)
        end4(1).wait_recv()
        second_only((2 * steps - LAG + 7) * HALF, HALF)

        for e in range(2):
            end1(e).wait_send()
            all_end(e2, e).wait_send()
            all_end(e3, e).wait_send()
            end4(e).wait_send()
        for m in MXUS:
            total = pltpu.matmul_pop(accs[m]["C"])
            for g in range(GROUPS // 2):
                prod_t[m * (GROUPS // 2) + g] = total[g * 128 : (g + 1) * 128, :128].T[:outs]

    def acc(m):
        of = pltpu.ACC(m)
        return {"A": [of((SEG, TILE), F32)] * RING, "B": of((outs, TILE), F32), "C": of((marks // 2, TILE), F32)}

    pl.run_scoped(main, [acc(m) for m in MXUS], [pltpu.VMEM((KEPT, 2, marks, TILE), BF16)] * 2)

    for k in range(GROUPS - 1):
        peer = (here + k + 1) % GROUPS
        along_pts(prod_t.at[peer], prod_in.at[k], o_send, o_recv, peer).start()

    def sent(b, carry):
        copy1(b).wait_send()
        all2(b).wait_send()
        all3(b).wait_send()
        copy4(b).wait_send()
        return carry

    lax.fori_loop(0, steps - 1, sent, 0)
    for i in range(2):
        along_pts(rows_in, rows_in, c_send.at[i], c_recv.at[i], here).wait_send()
    along_pts(prod_in, prod_in, o_send, o_recv, here).wait_recv()
    total = prod_t[here]
    for k in range(GROUPS - 1):
        total = total + prod_in[k]
    out[...] = total
    along_pts(prod_in, prod_in, o_send, o_recv, here).wait_send()


def per_device(points, landmark_ids, coefficients):
    pts_rows, width = points.shape
    marks, outs = coefficients.shape
    steps = pts_rows // STEP
    vmem = pl.BlockSpec(memory_space=pltpu.VMEM)
    dma = pltpu.SemaphoreType.DMA
    product = pl.pallas_call(
        functools.partial(body, steps),
        out_shape=jax.ShapeDtypeStruct((outs, marks // GROUPS), F32),
        in_specs=[pl.BlockSpec(memory_space=pltpu.SMEM), vmem, pl.BlockSpec(memory_space=pl.ANY)],
        out_specs=vmem,
        scratch_shapes=[
            pltpu.VMEM((pts_rows, width), BF16),
            pltpu.VMEM((steps, PIECES, TILE), F32),
            pltpu.VMEM((marks, width + 128), BF16),
            pltpu.VMEM((marks // GROUPS, width), F32),
            pltpu.VMEM((GROUPS, marks // GROUPS, width), BF16),
            pltpu.VMEM((GROUPS - 1, marks // GROUPS, width), BF16),
            pltpu.VMEM((GROUPS, marks // GROUPS, width), BF16),
            pltpu.VMEM((2, marks, TILE), BF16),
            pltpu.VMEM((2, marks, TILE), BF16),
            pltpu.VMEM((2 + steps * PIECES, outs, TILE), BF16),
            pltpu.VMEM((steps, GROUPS, outs, TILE), BF16),
            pltpu.VMEM((steps, GROUPS, outs, TILE), BF16),
            pltpu.VMEM((steps, GROUPS - 1, outs, TILE), BF16),
            pltpu.VMEM((BLANK + steps * PIECES, outs, TILE), BF16),
            pltpu.VMEM((2, GROUPS - 1, outs, 128), BF16),
            pltpu.VMEM((GROUPS, outs, 128), F32),
            pltpu.VMEM((GROUPS - 1, outs, 128), F32),
            dma((steps,)),
            dma((2,)),
            dma((2,)),
        ]
        + [dma((steps,))] * 8
        + [dma((2, 2))] * 4
        + [dma(()), dma(())],
        compiler_params=pltpu.CompilerParams(collective_id=0, has_side_effects=True, vmem_limit_bytes=60 * 2**20),
    )(landmark_ids, coefficients.T, points)
    return product.T / (pts_rows * GROUPS)


def solution(mesh):
    placed = (P("pts", None), P("lmk"), P("lmk", None))
    with jax.sharding.use_abstract_mesh(mesh.abstract_mesh):
        return jax.shard_map(
            per_device, mesh=mesh, in_specs=placed, out_specs=P(("lmk", "pts"), None), check_vma=False
        )
```

```python
import functools

import jax
import jax.numpy as jnp
from jax import lax
from jax.experimental import pallas as pl
from jax.experimental.pallas import tpu as pltpu
from jax.sharding import PartitionSpec as P

MESH = pl.DeviceIdType.MESH
BF16, F32 = jnp.bfloat16, jnp.float32
GROUPS = 8
TILE = 256
UNITS = 8
PIECES = 2 * UNITS
STEP = PIECES * TILE
HALF = UNITS // 2
LAG = 8
BACK = LAG * HALF + 3
KEPT = (BACK + 1) // 2
BLANK = 2 * (BACK - LAG * HALF)
SEG, RING = 64, 7
MXUS = (0, 1)


def augment(rows_f):
    sq = -0.25 * jnp.sum(rows_f * rows_f, axis=1, keepdims=True)
    hi = sq.astype(BF16).astype(F32)
    mid = (sq - hi).astype(BF16).astype(F32)
    low = sq - hi - mid
    lane = lax.broadcasted_iota(jnp.int32, rows_f.shape, 1)
    return jnp.where(lane == 0, hi, jnp.where(lane == 1, mid, jnp.where(lane == 2, low, 0.0))).astype(BF16)


def halves(rows):
    rows_f = rows.astype(F32)
    squares = rows_f * rows_f
    hi = squares.astype(BF16)
    return jnp.concatenate([hi, (squares - hi.astype(F32)).astype(BF16)], axis=1)


def body(steps, ids, ct, points, out, xm, sq, ca, picked_f, picked, rows_in, centers, pb0, pb1, part, p1r, p2s, p2r,
         fit, end_in, prod_t, prod_in, load_sem, c_send, c_recv, s1, r1, s2, r2, s3, r3, s4, r4, e1, e2, e3, e4, o_send, o_recv):
    here = lax.axis_index("pts")
    lmk = lax.axis_index("lmk")
    chip, core = lmk // 2, lmk % 2
    other = chip * 2 + 1 - core
    slab, width = xm.shape
    outs, marks = ct.shape
    pb = (pb0, pb1)

    def load(i):
        rows = pl.ds(i * STEP, STEP)
        return pltpu.make_async_copy(points.at[rows], xm.at[rows], load_sem.at[i])

    def start_load(i, carry):
        load(i).start()
        return carry

    lax.fori_loop(0, steps, start_load, 0)

    barrier = pltpu.get_barrier_semaphore()
    for k in range(GROUPS - 1):
        pl.semaphore_signal(barrier, inc=1, device_id={"pts": (here + k + 1) % GROUPS}, device_id_type=MESH)
        pl.semaphore_signal(barrier, inc=1, device_id={"lmk": ((chip + k + 1) % GROUPS) * 2 + core}, device_id_type=MESH)
    pl.semaphore_signal(barrier, inc=1, device_id={"lmk": other}, device_id_type=MESH)

    def along_pts(src, dst, send, recv, peer):
        return pltpu.make_async_remote_copy(src, dst, send, recv, device_id={"pts": peer}, device_id_type=MESH)

    def along_lmk(src, dst, send, recv, peer):
        return pltpu.make_async_remote_copy(src, dst, send, recv, device_id={"lmk": peer}, device_id_type=MESH)

    def gather(xf):
        def widen(i, carry):
            load(i).wait()
            for h in range(8):
                rows = pl.ds(i * STEP + h * (STEP // 8), STEP // 8)
                xf[rows, :] = xm[rows, :].astype(F32)
            return carry

        xf[pl.ds(slab, 8), :] = jnp.zeros((8, width), F32)
        lax.fori_loop(0, steps, widen, 0)

        def pick(k, carry):
            peer = (here + k + 1) % GROUPS

            def some(i, carry):
                for u in range(32):
                    row_at = i * 32 + u
                    at = ids[peer * 128 + row_at] - here * slab
                    at = jnp.where((at >= 0) & (at < slab), at, slab)
                    picked_f[pl.ds(row_at, 1), :] = xf[pl.ds(at, 1), :]
                return carry

            lax.fori_loop(0, 4, some, 0)
            picked[peer] = picked_f[...].astype(BF16)

            @pl.when(k < GROUPS - 1)
            def _():
                along_pts(picked.at[peer], rows_in.at[k], c_send.at[0], c_recv.at[0], peer).start()

            return carry

        pl.semaphore_wait(barrier, 2 * GROUPS - 1)
        lax.fori_loop(0, GROUPS, pick, 0)

    pl.run_scoped(gather, pltpu.VMEM((slab + 8, width), F32))

    def norms_of(low, high):
        def scoped(accs):
            quarter = jnp.full((32, TILE), -0.25, BF16)

            def some(i, carry):
                for h in range(0, PIECES, 4):
                    for q in range(h, h + 4):
                        rows = halves(xm[pl.ds(i * STEP + q * TILE, TILE), :])
                        pltpu.matmul_push_rhs(rows, q // 2 % 2, q % 2, transpose=True)
                        pltpu.matmul_acc_lhs(accs[q % 4], quarter, q // 2 % 2)
                    for q in range(h, h + 4):
                        sq[i, pl.ds(q, 1), :] = pltpu.matmul_pop(accs[q % 4])[:1]
                return carry

            lax.fori_loop(low, high, some, 0)

        pl.run_scoped(scoped, [pltpu.ACC(q % 2)((32, TILE), F32) for q in range(4)])

    norms_of(0, steps // 2)
    along_pts(rows_in, rows_in, c_send.at[0], c_recv.at[0], here).wait_recv()
    total = picked[here].astype(F32)
    for k in range(GROUPS - 1):
        total = total + rows_in[k].astype(F32)
    centers[here] = total.astype(BF16)
    for k in range(GROUPS - 1):
        peer = (here + k + 1) % GROUPS
        along_pts(centers.at[here], centers.at[here], c_send.at[1], c_recv.at[1], peer).start()
    norms_of(steps // 2, steps)
    pb1[...] = jnp.zeros_like(pb1)
    along_pts(rows_in, rows_in, c_send.at[1], c_recv.at[1], here).wait_recv()
    for g in range(GROUPS):
        rows_f = centers[g].astype(F32)
        ca[pl.ds(g * 128, 128), pl.ds(0, 128)] = (0.5 * rows_f).astype(BF16)
        ca[pl.ds(g * 128, 128), pl.ds(128, 128)] = augment(rows_f)

    def copy1(b):
        mine = part.at[pl.ds(2 + b * PIECES + (1 - core) * GROUPS, GROUPS)]
        return along_lmk(mine, p1r.at[b], s1.at[b], r1.at[b], other)

    def copy4(b):
        half = fit.at[pl.ds(BLANK + b * PIECES + core * GROUPS, GROUPS)]
        return along_lmk(half, half, s4.at[b], r4.at[b], other)

    def all2(b):
        return along_lmk(p2r.at[b], p2r.at[b], s2.at[b], r2.at[b], other)

    def all3(b):
        return along_lmk(p2r.at[b], p2r.at[b], s3.at[b], r3.at[b], other)

    def send1(b):
        copy1(b).start()

    def send2(b):
        copy1(b).wait_recv()
        for g in range(GROUPS):
            own = part[2 + b * PIECES + core * GROUPS + g]
            p2s[b, g] = (own.astype(F32) + p1r[b, g].astype(F32)).astype(BF16)
        for k in range(GROUPS - 1):
            peer = (chip + k + 1) % GROUPS
            along_lmk(p2s.at[b, peer], p2r.at[b, k], s2.at[b], r2.at[b], peer * 2 + core).start()

    def send3(b):
        all2(b).wait_recv()
        total = p2s[b, chip].astype(F32)
        for k in range(GROUPS - 1):
            total = total + p2r[b, k].astype(F32)
        mine = BLANK + b * PIECES + core * GROUPS + chip
        fit[mine] = total.astype(BF16)
        for k in range(GROUPS - 1):
            peer = (chip + k + 1) % GROUPS
            along_lmk(fit.at[mine], fit.at[mine], s3.at[b], r3.at[b], peer * 2 + core).start()

    def send4(b):
        all3(b).wait_recv()
        copy4(b).start()

    lane = lax.broadcasted_iota(jnp.int32, (TILE, 128), 1)
    ones = jnp.where(lane < 3, 1.0, 0.0).astype(BF16)
    blank = jnp.zeros((TILE - outs, TILE), BF16)
    segs = marks // SEG

    def main(accs, kts):
        def push_points(unit, m, reg):
            at = pl.multiple_of((unit * 2 + m) * TILE, TILE)
            rows = jnp.concatenate([xm[pl.ds(at, TILE), :], ones], axis=1)
            pltpu.matmul_push_rhs(rows, reg, m, transpose=True)

        def push_tile(par, m, q, reg):
            pltpu.matmul_push_rhs(pb[par][m, pl.ds(q * TILE, TILE), :], reg, m)

        def push_fitted(unit, c, m, reg):
            pltpu.matmul_push_rhs(jnp.concatenate([fit[BLANK + unit * 2 + c], blank], axis=0), reg, m, transpose=True)

        def first_product(unit, par, m, q, reg):
            acc = accs[m]["B"]
            pltpu.matmul_acc_lhs(acc, ct[:, pl.ds(q * TILE, TILE)], reg)
            if q == 3:
                part[unit * 2 + m] = pltpu.matmul_pop(acc).astype(BF16)

        def second_product(unit, par, c, m, reg):
            tile = kts[par][lax.rem(unit // 2 + KEPT, KEPT), c, pl.ds(m * (marks // 2), marks // 2), :]
            pltpu.matmul_acc_lhs(accs[m]["C"], tile, reg)

        def unit_step(h, i, par, second):
            unit = h * HALF + i
            slot = lax.rem(unit // 2, KEPT)
            after = jnp.minimum(unit + 1, steps * UNITS - 1)
            norms = [sq[unit // UNITS, pl.ds((unit % UNITS) * 2 + m, 1), :] for m in MXUS]

            def finish(m, s):
                tile = jnp.exp(pltpu.matmul_pop(accs[m]["A"][s % RING]) + norms[m]).astype(BF16)
                rows = pl.ds(s * SEG, SEG)
                kts[par][slot, m, rows, :] = tile
                pb[par][m, rows, :] = tile

            def distances(m, low, high):
                for s in range(low, high):
                    if s >= RING:
                        finish(m, s - RING)
                    acc = accs[m]["A"][s % RING]
                    pltpu.matmul_acc_lhs(acc, ca[pl.ds(s * SEG, SEG), :], 0 if s == low else None)

            def tail():
                for s in range(segs - RING, segs):
                    for m in MXUS:
                        finish(m, s)

            def each(f, *args):
                for m in MXUS:
                    f(*(m if a is MXUS else a for a in args))

            each(distances, MXUS, 0, segs // 2 if second else 3 * segs // 8)
            if second:
                before = unit - BACK
                each(push_fitted, before, 0, MXUS, 0)
                each(first_product, unit, par, MXUS, 0, 1)
                each(push_tile, 1 - par, MXUS, 1, 1)
                each(second_product, before, 1 - par, 0, MXUS, 0)
                each(push_points, unit, MXUS, 0)
                each(first_product, unit, par, MXUS, 1, 1)
                each(push_tile, 1 - par, MXUS, 2, 1)
                each(distances, MXUS, segs // 2, segs)
                each(push_fitted, before, 1, MXUS, 0)
                each(first_product, unit, par, MXUS, 2, 1)
                each(push_tile, 1 - par, MXUS, 3, 1)
                each(second_product, before, 1 - par, 1, MXUS, 0)
                tail()
                each(push_points, after, MXUS, 0)
                each(first_product, unit, par, MXUS, 3, 1)
                each(push_tile, par, MXUS, 0, 1)
            else:
                each(push_points, unit, MXUS, 0)
                each(first_product, unit, par, MXUS, 0, 1)
                each(push_tile, 1 - par, MXUS, 1, 1)
                each(distances, MXUS, 3 * segs // 8, 3 * segs // 4)
                each(push_points, unit, MXUS, 0)
                each(first_product, unit, par, MXUS, 1, 1)
                each(push_tile, 1 - par, MXUS, 2, 1)
                each(distances, MXUS, 3 * segs // 4, segs)
                each(push_tile, 1 - par, MXUS, 3, 0)
                each(first_product, unit, par, MXUS, 2, 1)
                tail()
                each(push_tile, par, MXUS, 0, 1)
                each(first_product, unit, par, MXUS, 3, 0)
                each(push_points, after, MXUS, 0)

        for m in MXUS:
            push_points(0, m, 0)
            push_tile(1, m, 0, 1)

        def exchange(h):
            for stage, behind in ((send2, 3), (send3, 5), (send4, 7)):
                due = (h % 2 == 1) & (h >= behind)
                pl.when(due)(functools.partial(stage, (h - behind) // 2))

        end = steps - 1
        lanes = pl.ds(pl.multiple_of(chip % 2 * 128, 128), 128)
        share = GROUPS // 2

        def end1(e):
            mine = part.at[pl.ds(2 + end * PIECES + e * GROUPS + (1 - core) * share, share)]
            return along_lmk(mine, p1r.at[end, pl.ds(e * share, share)], e1.at[0, e], e1.at[1, e], other)

        def all_end(stage, e):
            return along_lmk(end_in.at[e], end_in.at[e], stage.at[0, e], stage.at[1, e], other)

        def end4(e):
            half = fit.at[pl.ds(BLANK + end * PIECES + e * GROUPS + core * share, share)]
            return along_lmk(half, half, e4.at[0, e], e4.at[1, e], other)

        def end_send2(e):
            end1(e).wait_recv()
            for g in range(share):
                own = part[2 + end * PIECES + e * GROUPS + core * share + g]
                p2s[end, e * share + g] = (own.astype(F32) + p1r[end, e * share + g].astype(F32)).astype(BF16)
            for k in range(GROUPS - 1):
                peer = (chip + k + 1) % GROUPS
                theirs = pl.ds(pl.multiple_of(peer % 2 * 128, 128), 128)
                src = p2s.at[end, e * share + peer // 2, :, theirs]
                along_lmk(src, end_in.at[e, k], e2.at[0, e], e2.at[1, e], peer * 2 + core).start()

        def end_send3(e):
            all_end(e2, e).wait_recv()
            total = p2s[end, e * share + chip // 2, :, lanes].astype(F32)
            for k in range(GROUPS - 1):
                total = total + end_in[e, k].astype(F32)
            mine = BLANK + end * PIECES + e * GROUPS + core * share + chip // 2
            fit[mine, :, lanes] = total.astype(BF16)
            for k in range(GROUPS - 1):
                peer = (chip + k + 1) % GROUPS
                piece = fit.at[mine, :, lanes]
                along_lmk(piece, piece, e3.at[0, e], e3.at[1, e], peer * 2 + core).start()

        def end_send4(e):
            all_end(e3, e).wait_recv()
            end4(e).start()

        def tiles(low, high, second):
            def half(h, carry):
                def pair(i, carry):
                    @pl.when(((i == 1) & (h < 2 * steps - 1)) | ((i == 0) & (h == 2 * steps - 1)))
                    def _():
                        pl.when((h % 2 == 0) & (h >= 2))(functools.partial(send1, h // 2 - 1))
                        exchange(h)
                        if second:
                            pl.when(h % 2 == 0)(lambda: copy4((h - LAG) // 2).wait_recv())

                    if second:
                        pl.when((i == 1) & (h == 2 * steps - 1))(lambda: end1(0).start())
                    unit_step(h, i * 2, 0, second)
                    unit_step(h, i * 2 + 1, 1, second)
                    return carry

                return lax.fori_loop(0, HALF // 2, pair, carry)

            lax.fori_loop(low, high, half, 0)

        for unit in range(LAG * HALF - BACK, 0):
            kts[unit % 2][unit // 2 + KEPT] = jnp.zeros((2, marks, TILE), BF16)
        fit[pl.ds(0, BLANK)] = jnp.zeros((BLANK, outs, TILE), BF16)
        tiles(0, LAG, False)
        tiles(LAG, 2 * steps, True)

        def second_only(first, count):
            turns = [(first + i, (count + i) % 2, c) for i in range(count) for c in range(2)]
            for unit, _, c in turns[:2]:
                for m in MXUS:
                    push_fitted(unit, c, m, c)
            for at, (unit, par, c) in enumerate(turns):
                for m in MXUS:
                    second_product(unit, par, c, m, c)
                    if at + 2 < len(turns):
                        push_fitted(turns[at + 2][0], c, m, c)

        last = steps * UNITS
        for m in MXUS:
            pltpu.matmul_acc_lhs(accs[m]["A"][0], ca[pl.ds(0, SEG), :], 0)
            push_tile(1, m, 1, 0)
            first_product(last, 0, m, 0, 1)
            push_tile(1, m, 2, 1)
            first_product(last, 0, m, 1, 0)
            push_tile(1, m, 3, 0)
            first_product(last, 0, m, 2, 1)
            first_product(last, 0, m, 3, 0)
            pltpu.matmul_pop(accs[m]["A"][0])

        end1(1).start()
        end_send2(0)
        ahead = BACK - LAG * HALF
        second_only((2 * steps - LAG) * HALF - ahead, ahead)
        end_send2(1)
        copy4(end - 3).wait_recv()
        second_only((2 * steps - LAG) * HALF, HALF)
        send3(end - 1)
        send4(end - 2)
        second_only((2 * steps - LAG + 1) * HALF, HALF)
        copy4(end - 2).wait_recv()
        second_only((2 * steps - LAG + 2) * HALF, HALF)
        end_send3(0)
        end_send3(1)
        second_only((2 * steps - LAG + 3) * HALF, HALF)
        send4(end - 1)
        copy4(end - 1).wait_recv()
        second_only((2 * steps - LAG + 4) * HALF, HALF)
        end_send4(0)
        second_only((2 * steps - LAG + 5) * HALF, HALF)
        end_send4(1)
        end4(0).wait_recv()
        second_only((2 * steps - LAG + 6) * HALF, HALF)
        end4(1).wait_recv()
        second_only((2 * steps - LAG + 7) * HALF, HALF)

        for e in range(2):
            end1(e).wait_send()
            all_end(e2, e).wait_send()
            all_end(e3, e).wait_send()
            end4(e).wait_send()
        for m in MXUS:
            total = pltpu.matmul_pop(accs[m]["C"])
            for g in range(GROUPS // 2):
                prod_t[m * (GROUPS // 2) + g] = total[g * 128 : (g + 1) * 128, :128].T[:outs]

    def acc(m):
        of = pltpu.ACC(m)
        return {"A": [of((SEG, TILE), F32)] * RING, "B": of((outs, TILE), F32), "C": of((marks // 2, TILE), F32)}

    pl.run_scoped(main, [acc(m) for m in MXUS], [pltpu.VMEM((KEPT, 2, marks, TILE), BF16)] * 2)

    for k in range(GROUPS - 1):
        peer = (here + k + 1) % GROUPS
        along_pts(prod_t.at[peer], prod_in.at[k], o_send, o_recv, peer).start()

    def sent(b, carry):
        copy1(b).wait_send()
        all2(b).wait_send()
        all3(b).wait_send()
        copy4(b).wait_send()
        return carry

    lax.fori_loop(0, steps - 1, sent, 0)
    for i in range(2):
        along_pts(rows_in, rows_in, c_send.at[i], c_recv.at[i], here).wait_send()
    along_pts(prod_in, prod_in, o_send, o_recv, here).wait_recv()
    total = prod_t[here]
    for k in range(GROUPS - 1):
        total = total + prod_in[k]
    out[...] = total
    along_pts(prod_in, prod_in, o_send, o_recv, here).wait_send()


def per_device(points, landmark_ids, coefficients):
    pts_rows, width = points.shape
    marks, outs = coefficients.shape
    steps = pts_rows // STEP
    vmem = pl.BlockSpec(memory_space=pltpu.VMEM)
    dma = pltpu.SemaphoreType.DMA
    product = pl.pallas_call(
        functools.partial(body, steps),
        out_shape=jax.ShapeDtypeStruct((outs, marks // GROUPS), F32),
        in_specs=[pl.BlockSpec(memory_space=pltpu.SMEM), vmem, pl.BlockSpec(memory_space=pl.ANY)],
        out_specs=vmem,
        scratch_shapes=[
            pltpu.VMEM((pts_rows, width), BF16),
            pltpu.VMEM((steps, PIECES, TILE), F32),
            pltpu.VMEM((marks, width + 128), BF16),
            pltpu.VMEM((marks // GROUPS, width), F32),
            pltpu.VMEM((GROUPS, marks // GROUPS, width), BF16),
            pltpu.VMEM((GROUPS - 1, marks // GROUPS, width), BF16),
            pltpu.VMEM((GROUPS, marks // GROUPS, width), BF16),
            pltpu.VMEM((2, marks, TILE), BF16),
            pltpu.VMEM((2, marks, TILE), BF16),
            pltpu.VMEM((2 + steps * PIECES, outs, TILE), BF16),
            pltpu.VMEM((steps, GROUPS, outs, TILE), BF16),
            pltpu.VMEM((steps, GROUPS, outs, TILE), BF16),
            pltpu.VMEM((steps, GROUPS - 1, outs, TILE), BF16),
            pltpu.VMEM((BLANK + steps * PIECES, outs, TILE), BF16),
            pltpu.VMEM((2, GROUPS - 1, outs, 128), BF16),
            pltpu.VMEM((GROUPS, outs, 128), F32),
            pltpu.VMEM((GROUPS - 1, outs, 128), F32),
            dma((steps,)),
            dma((2,)),
            dma((2,)),
        ]
        + [dma((steps,))] * 8
        + [dma((2, 2))] * 4
        + [dma(()), dma(())],
        compiler_params=pltpu.CompilerParams(collective_id=0, has_side_effects=True, vmem_limit_bytes=60 * 2**20),
    )(landmark_ids, coefficients.T, points)
    return product.T / (pts_rows * GROUPS)


def solution(mesh):
    placed = (P("pts", None), P("lmk"), P("lmk", None))
    with jax.sharding.use_abstract_mesh(mesh.abstract_mesh):
        return jax.shard_map(
            per_device, mesh=mesh, in_specs=placed, out_specs=P(("lmk", "pts"), None), check_vma=False
        )
```

```python
import functools

import jax
import jax.numpy as jnp
from jax import lax
from jax.experimental import pallas as pl
from jax.experimental.pallas import tpu as pltpu
from jax.sharding import PartitionSpec as P

MESH = pl.DeviceIdType.MESH
BF16, F32 = jnp.bfloat16, jnp.float32
GROUPS = 8
TILE = 256
UNITS = 8
PIECES = 2 * UNITS
STEP = PIECES * TILE
HALF = UNITS // 2
LAG = 8
BACK = LAG * HALF + 3
KEPT = (BACK + 1) // 2
BLANK = 2 * (BACK - LAG * HALF)
SEG, RING = 64, 7
MXUS = (0, 1)


def augment(rows_f):
    sq = -0.25 * jnp.sum(rows_f * rows_f, axis=1, keepdims=True)
    hi = sq.astype(BF16).astype(F32)
    mid = (sq - hi).astype(BF16).astype(F32)
    low = sq - hi - mid
    lane = lax.broadcasted_iota(jnp.int32, rows_f.shape, 1)
    return jnp.where(lane == 0, hi, jnp.where(lane == 1, mid, jnp.where(lane == 2, low, 0.0))).astype(BF16)


def halves(rows):
    rows_f = rows.astype(F32)
    squares = rows_f * rows_f
    hi = squares.astype(BF16)
    return jnp.concatenate([hi, (squares - hi.astype(F32)).astype(BF16)], axis=1)


def body(steps, ids, ct, points, out, xm, sq, ca, picked_f, picked, rows_in, centers, pb0, pb1, part, p1r, p2s, p2r,
         fit, end_in, prod_t, prod_in, load_sem, c_send, c_recv, s1, r1, s2, r2, s3, r3, s4, r4, e1, e2, e3, e4, o_send, o_recv):
    here = lax.axis_index("pts")
    lmk = lax.axis_index("lmk")
    chip, core = lmk // 2, lmk % 2
    other = chip * 2 + 1 - core
    slab, width = xm.shape
    outs, marks = ct.shape
    pb = (pb0, pb1)

    def load(i):
        rows = pl.ds(i * STEP, STEP)
        return pltpu.make_async_copy(points.at[rows], xm.at[rows], load_sem.at[i])

    def start_load(i, carry):
        load(i).start()
        return carry

    lax.fori_loop(0, steps, start_load, 0)

    barrier = pltpu.get_barrier_semaphore()
    for k in range(GROUPS - 1):
        pl.semaphore_signal(barrier, inc=1, device_id={"pts": (here + k + 1) % GROUPS}, device_id_type=MESH)
        pl.semaphore_signal(barrier, inc=1, device_id={"lmk": ((chip + k + 1) % GROUPS) * 2 + core}, device_id_type=MESH)
    pl.semaphore_signal(barrier, inc=1, device_id={"lmk": other}, device_id_type=MESH)

    def along_pts(src, dst, send, recv, peer):
        return pltpu.make_async_remote_copy(src, dst, send, recv, device_id={"pts": peer}, device_id_type=MESH)

    def along_lmk(src, dst, send, recv, peer):
        return pltpu.make_async_remote_copy(src, dst, send, recv, device_id={"lmk": peer}, device_id_type=MESH)

    def gather(xf):
        def widen(i, carry):
            load(i).wait()
            for h in range(8):
                rows = pl.ds(i * STEP + h * (STEP // 8), STEP // 8)
                xf[rows, :] = xm[rows, :].astype(F32)
            return carry

        xf[pl.ds(slab, 8), :] = jnp.zeros((8, width), F32)
        lax.fori_loop(0, steps, widen, 0)

        def pick(k, carry):
            peer = (here + k + 1) % GROUPS

            def some(i, carry):
                for u in range(32):
                    row_at = i * 32 + u
                    at = ids[peer * 128 + row_at] - here * slab
                    at = jnp.where((at >= 0) & (at < slab), at, slab)
                    picked_f[pl.ds(row_at, 1), :] = xf[pl.ds(at, 1), :]
                return carry

            lax.fori_loop(0, 4, some, 0)
            picked[peer] = picked_f[...].astype(BF16)

            @pl.when(k < GROUPS - 1)
            def _():
                along_pts(picked.at[peer], rows_in.at[k], c_send.at[0], c_recv.at[0], peer).start()

            return carry

        pl.semaphore_wait(barrier, 2 * GROUPS - 1)
        lax.fori_loop(0, GROUPS, pick, 0)

    pl.run_scoped(gather, pltpu.VMEM((slab + 8, width), F32))

    def norms_of(low, high):
        def scoped(accs):
            quarter = jnp.full((32, TILE), -0.25, BF16)

            def some(i, carry):
                for h in range(0, PIECES, 4):
                    for q in range(h, h + 4):
                        rows = halves(xm[pl.ds(i * STEP + q * TILE, TILE), :])
                        pltpu.matmul_push_rhs(rows, q // 2 % 2, q % 2, transpose=True)
                        pltpu.matmul_acc_lhs(accs[q % 4], quarter, q // 2 % 2)
                    for q in range(h, h + 4):
                        sq[i, pl.ds(q, 1), :] = pltpu.matmul_pop(accs[q % 4])[:1]
                return carry

            lax.fori_loop(low, high, some, 0)

        pl.run_scoped(scoped, [pltpu.ACC(q % 2)((32, TILE), F32) for q in range(4)])

    norms_of(0, steps // 4)
    along_pts(rows_in, rows_in, c_send.at[0], c_recv.at[0], here).wait_recv()
    total = picked[here].astype(F32)
    for k in range(GROUPS - 1):
        total = total + rows_in[k].astype(F32)
    centers[here] = total.astype(BF16)
    for k in range(GROUPS - 1):
        peer = (here + k + 1) % GROUPS
        along_pts(centers.at[here], centers.at[here], c_send.at[1], c_recv.at[1], peer).start()
    norms_of(steps // 4, steps)
    pb1[...] = jnp.zeros_like(pb1)
    along_pts(rows_in, rows_in, c_send.at[1], c_recv.at[1], here).wait_recv()
    for g in range(GROUPS):
        rows_f = centers[g].astype(F32)
        ca[pl.ds(g * 128, 128), pl.ds(0, 128)] = (0.5 * rows_f).astype(BF16)
        ca[pl.ds(g * 128, 128), pl.ds(128, 128)] = augment(rows_f)

    def copy1(b):
        mine = part.at[pl.ds(2 + b * PIECES + (1 - core) * GROUPS, GROUPS)]
        return along_lmk(mine, p1r.at[b], s1.at[b], r1.at[b], other)

    def copy4(b):
        half = fit.at[pl.ds(BLANK + b * PIECES + core * GROUPS, GROUPS)]
        return along_lmk(half, half, s4.at[b], r4.at[b], other)

    def all2(b):
        return along_lmk(p2r.at[b], p2r.at[b], s2.at[b], r2.at[b], other)

    def all3(b):
        return along_lmk(p2r.at[b], p2r.at[b], s3.at[b], r3.at[b], other)

    def send1(b):
        copy1(b).start()

    def send2(b):
        copy1(b).wait_recv()
        for g in range(GROUPS):
            own = part[2 + b * PIECES + core * GROUPS + g]
            p2s[b, g] = (own.astype(F32) + p1r[b, g].astype(F32)).astype(BF16)
        for k in range(GROUPS - 1):
            peer = (chip + k + 1) % GROUPS
            along_lmk(p2s.at[b, peer], p2r.at[b, k], s2.at[b], r2.at[b], peer * 2 + core).start()

    def send3(b):
        all2(b).wait_recv()
        total = p2s[b, chip].astype(F32)
        for k in range(GROUPS - 1):
            total = total + p2r[b, k].astype(F32)
        mine = BLANK + b * PIECES + core * GROUPS + chip
        fit[mine] = total.astype(BF16)
        for k in range(GROUPS - 1):
            peer = (chip + k + 1) % GROUPS
            along_lmk(fit.at[mine], fit.at[mine], s3.at[b], r3.at[b], peer * 2 + core).start()

    def send4(b):
        all3(b).wait_recv()
        copy4(b).start()

    lane = lax.broadcasted_iota(jnp.int32, (TILE, 128), 1)
    ones = jnp.where(lane < 3, 1.0, 0.0).astype(BF16)
    blank = jnp.zeros((TILE - outs, TILE), BF16)
    segs = marks // SEG

    def main(accs, kts):
        def push_points(unit, m, reg):
            at = pl.multiple_of((unit * 2 + m) * TILE, TILE)
            rows = jnp.concatenate([xm[pl.ds(at, TILE), :], ones], axis=1)
            pltpu.matmul_push_rhs(rows, reg, m, transpose=True)

        def push_tile(par, m, q, reg):
            pltpu.matmul_push_rhs(pb[par][m, pl.ds(q * TILE, TILE), :], reg, m)

        def push_fitted(unit, c, m, reg):
            pltpu.matmul_push_rhs(jnp.concatenate([fit[BLANK + unit * 2 + c], blank], axis=0), reg, m, transpose=True)

        def first_product(unit, par, m, q, reg):
            acc = accs[m]["B"]
            pltpu.matmul_acc_lhs(acc, ct[:, pl.ds(q * TILE, TILE)], reg)
            if q == 3:
                part[unit * 2 + m] = pltpu.matmul_pop(acc).astype(BF16)

        def second_product(unit, par, c, m, reg):
            tile = kts[par][lax.rem(unit // 2 + KEPT, KEPT), c, pl.ds(m * (marks // 2), marks // 2), :]
            pltpu.matmul_acc_lhs(accs[m]["C"], tile, reg)

        def unit_step(h, i, par, second):
            unit = h * HALF + i
            slot = lax.rem(unit // 2, KEPT)
            after = jnp.minimum(unit + 1, steps * UNITS - 1)
            norms = [sq[unit // UNITS, pl.ds((unit % UNITS) * 2 + m, 1), :] for m in MXUS]

            def finish(m, s):
                tile = jnp.exp(pltpu.matmul_pop(accs[m]["A"][s % RING]) + norms[m]).astype(BF16)
                rows = pl.ds(s * SEG, SEG)
                kts[par][slot, m, rows, :] = tile
                pb[par][m, rows, :] = tile

            def distances(m, low, high):
                for s in range(low, high):
                    if s >= RING:
                        finish(m, s - RING)
                    acc = accs[m]["A"][s % RING]
                    pltpu.matmul_acc_lhs(acc, ca[pl.ds(s * SEG, SEG), :], 0 if s == low else None)

            def tail():
                for s in range(segs - RING, segs):
                    for m in MXUS:
                        finish(m, s)

            def each(f, *args):
                for m in MXUS:
                    f(*(m if a is MXUS else a for a in args))

            each(distances, MXUS, 0, segs // 2 if second else 3 * segs // 8)
            if second:
                before = unit - BACK
                each(push_fitted, before, 0, MXUS, 0)
                each(first_product, unit, par, MXUS, 0, 1)
                each(push_tile, 1 - par, MXUS, 1, 1)
                each(second_product, before, 1 - par, 0, MXUS, 0)
                each(push_points, unit, MXUS, 0)
                each(first_product, unit, par, MXUS, 1, 1)
                each(push_tile, 1 - par, MXUS, 2, 1)
                each(distances, MXUS, segs // 2, segs)
                each(push_fitted, before, 1, MXUS, 0)
                each(first_product, unit, par, MXUS, 2, 1)
                each(push_tile, 1 - par, MXUS, 3, 1)
                each(second_product, before, 1 - par, 1, MXUS, 0)
                tail()
                each(push_points, after, MXUS, 0)
                each(first_product, unit, par, MXUS, 3, 1)
                each(push_tile, par, MXUS, 0, 1)
            else:
                each(push_points, unit, MXUS, 0)
                each(first_product, unit, par, MXUS, 0, 1)
                each(push_tile, 1 - par, MXUS, 1, 1)
                each(distances, MXUS, 3 * segs // 8, 3 * segs // 4)
                each(push_points, unit, MXUS, 0)
                each(first_product, unit, par, MXUS, 1, 1)
                each(push_tile, 1 - par, MXUS, 2, 1)
                each(distances, MXUS, 3 * segs // 4, segs)
                each(push_tile, 1 - par, MXUS, 3, 0)
                each(first_product, unit, par, MXUS, 2, 1)
                tail()
                each(push_tile, par, MXUS, 0, 1)
                each(first_product, unit, par, MXUS, 3, 0)
                each(push_points, after, MXUS, 0)

        for m in MXUS:
            push_points(0, m, 0)
            push_tile(1, m, 0, 1)

        def exchange(h):
            for stage, behind in ((send2, 3), (send3, 5), (send4, 7)):
                due = (h % 2 == 1) & (h >= behind)
                pl.when(due)(functools.partial(stage, (h - behind) // 2))

        end = steps - 1
        lanes = pl.ds(pl.multiple_of(chip % 2 * 128, 128), 128)
        share = GROUPS // 2

        def end1(e):
            mine = part.at[pl.ds(2 + end * PIECES + e * GROUPS + (1 - core) * share, share)]
            return along_lmk(mine, p1r.at[end, pl.ds(e * share, share)], e1.at[0, e], e1.at[1, e], other)

        def all_end(stage, e):
            return along_lmk(end_in.at[e], end_in.at[e], stage.at[0, e], stage.at[1, e], other)

        def end4(e):
            half = fit.at[pl.ds(BLANK + end * PIECES + e * GROUPS + core * share, share)]
            return along_lmk(half, half, e4.at[0, e], e4.at[1, e], other)

        def end_send2(e):
            end1(e).wait_recv()
            for g in range(share):
                own = part[2 + end * PIECES + e * GROUPS + core * share + g]
                p2s[end, e * share + g] = (own.astype(F32) + p1r[end, e * share + g].astype(F32)).astype(BF16)
            for k in range(GROUPS - 1):
                peer = (chip + k + 1) % GROUPS
                theirs = pl.ds(pl.multiple_of(peer % 2 * 128, 128), 128)
                src = p2s.at[end, e * share + peer // 2, :, theirs]
                along_lmk(src, end_in.at[e, k], e2.at[0, e], e2.at[1, e], peer * 2 + core).start()

        def end_send3(e):
            all_end(e2, e).wait_recv()
            total = p2s[end, e * share + chip // 2, :, lanes].astype(F32)
            for k in range(GROUPS - 1):
                total = total + end_in[e, k].astype(F32)
            mine = BLANK + end * PIECES + e * GROUPS + core * share + chip // 2
            fit[mine, :, lanes] = total.astype(BF16)
            for k in range(GROUPS - 1):
                peer = (chip + k + 1) % GROUPS
                piece = fit.at[mine, :, lanes]
                along_lmk(piece, piece, e3.at[0, e], e3.at[1, e], peer * 2 + core).start()

        def end_send4(e):
            all_end(e3, e).wait_recv()
            end4(e).start()

        def tiles(low, high, second):
            def half(h, carry):
                def pair(i, carry):
                    @pl.when(((i == 1) & (h < 2 * steps - 1)) | ((i == 0) & (h == 2 * steps - 1)))
                    def _():
                        pl.when((h % 2 == 0) & (h >= 2))(functools.partial(send1, h // 2 - 1))
                        exchange(h)
                        if second:
                            pl.when(h % 2 == 0)(lambda: copy4((h - LAG) // 2).wait_recv())

                    if second:
                        pl.when((i == 1) & (h == 2 * steps - 1))(lambda: end1(0).start())
                    unit_step(h, i * 2, 0, second)
                    unit_step(h, i * 2 + 1, 1, second)
                    return carry

                return lax.fori_loop(0, HALF // 2, pair, carry)

            lax.fori_loop(low, high, half, 0)

        for unit in range(LAG * HALF - BACK, 0):
            kts[unit % 2][unit // 2 + KEPT] = jnp.zeros((2, marks, TILE), BF16)
        fit[pl.ds(0, BLANK)] = jnp.zeros((BLANK, outs, TILE), BF16)
        tiles(0, LAG, False)
        tiles(LAG, 2 * steps, True)

        def second_only(first, count):
            turns = [(first + i, (count + i) % 2, c) for i in range(count) for c in range(2)]
            for unit, _, c in turns[:2]:
                for m in MXUS:
                    push_fitted(unit, c, m, c)
            for at, (unit, par, c) in enumerate(turns):
                for m in MXUS:
                    second_product(unit, par, c, m, c)
                    if at + 2 < len(turns):
                        push_fitted(turns[at + 2][0], c, m, c)

        last = steps * UNITS
        for m in MXUS:
            pltpu.matmul_acc_lhs(accs[m]["A"][0], ca[pl.ds(0, SEG), :], 0)
            push_tile(1, m, 1, 0)
            first_product(last, 0, m, 0, 1)
            push_tile(1, m, 2, 1)
            first_product(last, 0, m, 1, 0)
            push_tile(1, m, 3, 0)
            first_product(last, 0, m, 2, 1)
            first_product(last, 0, m, 3, 0)
            pltpu.matmul_pop(accs[m]["A"][0])

        end1(1).start()
        end_send2(0)
        ahead = BACK - LAG * HALF
        second_only((2 * steps - LAG) * HALF - ahead, ahead)
        end_send2(1)
        copy4(end - 3).wait_recv()
        second_only((2 * steps - LAG) * HALF, HALF)
        send3(end - 1)
        send4(end - 2)
        second_only((2 * steps - LAG + 1) * HALF, HALF)
        copy4(end - 2).wait_recv()
        second_only((2 * steps - LAG + 2) * HALF, HALF)
        end_send3(0)
        second_only((2 * steps - LAG + 3) * HALF, HALF)
        end_send3(1)
        send4(end - 1)
        copy4(end - 1).wait_recv()
        second_only((2 * steps - LAG + 4) * HALF, HALF)
        end_send4(0)
        second_only((2 * steps - LAG + 5) * HALF, HALF)
        end_send4(1)
        end4(0).wait_recv()
        second_only((2 * steps - LAG + 6) * HALF, HALF)
        end4(1).wait_recv()
        second_only((2 * steps - LAG + 7) * HALF, HALF)

        for e in range(2):
            end1(e).wait_send()
            all_end(e2, e).wait_send()
            all_end(e3, e).wait_send()
            end4(e).wait_send()
        for m in MXUS:
            total = pltpu.matmul_pop(accs[m]["C"])
            for g in range(GROUPS // 2):
                prod_t[m * (GROUPS // 2) + g] = total[g * 128 : (g + 1) * 128, :128].T[:outs]

    def acc(m):
        of = pltpu.ACC(m)
        return {"A": [of((SEG, TILE), F32)] * RING, "B": of((outs, TILE), F32), "C": of((marks // 2, TILE), F32)}

    pl.run_scoped(main, [acc(m) for m in MXUS], [pltpu.VMEM((KEPT, 2, marks, TILE), BF16)] * 2)

    for k in range(GROUPS - 1):
        peer = (here + k + 1) % GROUPS
        along_pts(prod_t.at[peer], prod_in.at[k], o_send, o_recv, peer).start()

    def sent(b, carry):
        copy1(b).wait_send()
        all2(b).wait_send()
        all3(b).wait_send()
        copy4(b).wait_send()
        return carry

    lax.fori_loop(0, steps - 1, sent, 0)
    for i in range(2):
        along_pts(rows_in, rows_in, c_send.at[i], c_recv.at[i], here).wait_send()
    along_pts(prod_in, prod_in, o_send, o_recv, here).wait_recv()
    total = prod_t[here]
    for k in range(GROUPS - 1):
        total = total + prod_in[k]
    out[...] = total
    along_pts(prod_in, prod_in, o_send, o_recv, here).wait_send()


def per_device(points, landmark_ids, coefficients):
    pts_rows, width = points.shape
    marks, outs = coefficients.shape
    steps = pts_rows // STEP
    vmem = pl.BlockSpec(memory_space=pltpu.VMEM)
    dma = pltpu.SemaphoreType.DMA
    product = pl.pallas_call(
        functools.partial(body, steps),
        out_shape=jax.ShapeDtypeStruct((outs, marks // GROUPS), F32),
        in_specs=[pl.BlockSpec(memory_space=pltpu.SMEM), vmem, pl.BlockSpec(memory_space=pl.ANY)],
        out_specs=vmem,
        scratch_shapes=[
            pltpu.VMEM((pts_rows, width), BF16),
            pltpu.VMEM((steps, PIECES, TILE), F32),
            pltpu.VMEM((marks, width + 128), BF16),
            pltpu.VMEM((marks // GROUPS, width), F32),
            pltpu.VMEM((GROUPS, marks // GROUPS, width), BF16),
            pltpu.VMEM((GROUPS - 1, marks // GROUPS, width), BF16),
            pltpu.VMEM((GROUPS, marks // GROUPS, width), BF16),
            pltpu.VMEM((2, marks, TILE), BF16),
            pltpu.VMEM((2, marks, TILE), BF16),
            pltpu.VMEM((2 + steps * PIECES, outs, TILE), BF16),
            pltpu.VMEM((steps, GROUPS, outs, TILE), BF16),
            pltpu.VMEM((steps, GROUPS, outs, TILE), BF16),
            pltpu.VMEM((steps, GROUPS - 1, outs, TILE), BF16),
            pltpu.VMEM((BLANK + steps * PIECES, outs, TILE), BF16),
            pltpu.VMEM((2, GROUPS - 1, outs, 128), BF16),
            pltpu.VMEM((GROUPS, outs, 128), F32),
            pltpu.VMEM((GROUPS - 1, outs, 128), F32),
            dma((steps,)),
            dma((2,)),
            dma((2,)),
        ]
        + [dma((steps,))] * 8
        + [dma((2, 2))] * 4
        + [dma(()), dma(())],
        compiler_params=pltpu.CompilerParams(collective_id=0, has_side_effects=True, vmem_limit_bytes=60 * 2**20),
    )(landmark_ids, coefficients.T, points)
    return product.T / (pts_rows * GROUPS)


def solution(mesh):
    placed = (P("pts", None), P("lmk"), P("lmk", None))
    with jax.sharding.use_abstract_mesh(mesh.abstract_mesh):
        return jax.shard_map(
            per_device, mesh=mesh, in_specs=placed, out_specs=P(("lmk", "pts"), None), check_vma=False
        )
```

```python
import functools

import jax
import jax.numpy as jnp
from jax import lax
from jax.experimental import pallas as pl
from jax.experimental.pallas import tpu as pltpu
from jax.sharding import PartitionSpec as P

MESH = pl.DeviceIdType.MESH
BF16, F32 = jnp.bfloat16, jnp.float32
GROUPS = 8
TILE = 256
UNITS = 8
PIECES = 2 * UNITS
STEP = PIECES * TILE
HALF = UNITS // 2
LAG = 8
BACK = LAG * HALF + 3
KEPT = (BACK + 1) // 2
BLANK = 2 * (BACK - LAG * HALF)
SEG, RING = 64, 7
MXUS = (0, 1)


def augment(rows_f):
    sq = -0.25 * jnp.sum(rows_f * rows_f, axis=1, keepdims=True)
    hi = sq.astype(BF16).astype(F32)
    mid = (sq - hi).astype(BF16).astype(F32)
    low = sq - hi - mid
    lane = lax.broadcasted_iota(jnp.int32, rows_f.shape, 1)
    return jnp.where(lane == 0, hi, jnp.where(lane == 1, mid, jnp.where(lane == 2, low, 0.0))).astype(BF16)


def halves(rows):
    rows_f = rows.astype(F32)
    squares = rows_f * rows_f
    hi = squares.astype(BF16)
    return jnp.concatenate([hi, (squares - hi.astype(F32)).astype(BF16)], axis=1)


def body(steps, ids, ct, points, out, xm, sq, ca, picked_f, picked, rows_in, centers, pb0, pb1, part, p1r, p2s, p2r,
         fit, end_in, prod_t, prod_in, load_sem, c_send, c_recv, s1, r1, s2, r2, s3, r3, s4, r4, e1, e2, e3, e4, o_send, o_recv):
    here = lax.axis_index("pts")
    lmk = lax.axis_index("lmk")
    chip, core = lmk // 2, lmk % 2
    other = chip * 2 + 1 - core
    slab, width = xm.shape
    outs, marks = ct.shape
    pb = (pb0, pb1)

    def load(i):
        rows = pl.ds(i * STEP, STEP)
        return pltpu.make_async_copy(points.at[rows], xm.at[rows], load_sem.at[i])

    def start_load(i, carry):
        load(i).start()
        return carry

    lax.fori_loop(0, steps, start_load, 0)

    barrier = pltpu.get_barrier_semaphore()
    for k in range(GROUPS - 1):
        pl.semaphore_signal(barrier, inc=1, device_id={"pts": (here + k + 1) % GROUPS}, device_id_type=MESH)
        pl.semaphore_signal(barrier, inc=1, device_id={"lmk": ((chip + k + 1) % GROUPS) * 2 + core}, device_id_type=MESH)
    pl.semaphore_signal(barrier, inc=1, device_id={"lmk": other}, device_id_type=MESH)

    def along_pts(src, dst, send, recv, peer):
        return pltpu.make_async_remote_copy(src, dst, send, recv, device_id={"pts": peer}, device_id_type=MESH)

    def along_lmk(src, dst, send, recv, peer):
        return pltpu.make_async_remote_copy(src, dst, send, recv, device_id={"lmk": peer}, device_id_type=MESH)

    def gather(xf):
        def widen(i, carry):
            load(i).wait()
            for h in range(8):
                rows = pl.ds(i * STEP + h * (STEP // 8), STEP // 8)
                xf[rows, :] = xm[rows, :].astype(F32)
            return carry

        xf[pl.ds(slab, 8), :] = jnp.zeros((8, width), F32)
        lax.fori_loop(0, steps, widen, 0)

        def pick(k, carry):
            peer = (here + k + 1) % GROUPS

            def some(i, carry):
                for u in range(64):
                    row_at = i * 64 + u
                    at = ids[peer * 128 + row_at] - here * slab
                    at = jnp.where((at >= 0) & (at < slab), at, slab)
                    picked_f[pl.ds(row_at, 1), :] = xf[pl.ds(at, 1), :]
                return carry

            lax.fori_loop(0, 2, some, 0)
            picked[peer] = picked_f[...].astype(BF16)

            @pl.when(k < GROUPS - 1)
            def _():
                along_pts(picked.at[peer], rows_in.at[k], c_send.at[0], c_recv.at[0], peer).start()

            return carry

        pl.semaphore_wait(barrier, 2 * GROUPS - 1)
        lax.fori_loop(0, GROUPS, pick, 0)

    pl.run_scoped(gather, pltpu.VMEM((slab + 8, width), F32))

    def norms_of(low, high):
        def scoped(accs):
            quarter = jnp.full((32, TILE), -0.25, BF16)

            def some(i, carry):
                for h in range(0, PIECES, 4):
                    for q in range(h, h + 4):
                        rows = halves(xm[pl.ds(i * STEP + q * TILE, TILE), :])
                        pltpu.matmul_push_rhs(rows, q // 2 % 2, q % 2, transpose=True)
                        pltpu.matmul_acc_lhs(accs[q % 4], quarter, q // 2 % 2)
                    for q in range(h, h + 4):
                        sq[i, pl.ds(q, 1), :] = pltpu.matmul_pop(accs[q % 4])[:1]
                return carry

            lax.fori_loop(low, high, some, 0)

        pl.run_scoped(scoped, [pltpu.ACC(q % 2)((32, TILE), F32) for q in range(4)])

    norms_of(0, steps // 4)
    along_pts(rows_in, rows_in, c_send.at[0], c_recv.at[0], here).wait_recv()
    total = picked[here].astype(F32)
    for k in range(GROUPS - 1):
        total = total + rows_in[k].astype(F32)
    centers[here] = total.astype(BF16)
    for k in range(GROUPS - 1):
        peer = (here + k + 1) % GROUPS
        along_pts(centers.at[here], centers.at[here], c_send.at[1], c_recv.at[1], peer).start()
    norms_of(steps // 4, steps)
    pb1[...] = jnp.zeros_like(pb1)
    along_pts(rows_in, rows_in, c_send.at[1], c_recv.at[1], here).wait_recv()
    for g in range(GROUPS):
        rows_f = centers[g].astype(F32)
        ca[pl.ds(g * 128, 128), pl.ds(0, 128)] = (0.5 * rows_f).astype(BF16)
        ca[pl.ds(g * 128, 128), pl.ds(128, 128)] = augment(rows_f)

    def copy1(b):
        mine = part.at[pl.ds(2 + b * PIECES + (1 - core) * GROUPS, GROUPS)]
        return along_lmk(mine, p1r.at[b], s1.at[b], r1.at[b], other)

    def copy4(b):
        half = fit.at[pl.ds(BLANK + b * PIECES + core * GROUPS, GROUPS)]
        return along_lmk(half, half, s4.at[b], r4.at[b], other)

    def all2(b):
        return along_lmk(p2r.at[b], p2r.at[b], s2.at[b], r2.at[b], other)

    def all3(b):
        return along_lmk(p2r.at[b], p2r.at[b], s3.at[b], r3.at[b], other)

    def send1(b):
        copy1(b).start()

    def send2(b):
        copy1(b).wait_recv()
        for g in range(GROUPS):
            own = part[2 + b * PIECES + core * GROUPS + g]
            p2s[b, g] = (own.astype(F32) + p1r[b, g].astype(F32)).astype(BF16)
        for k in range(GROUPS - 1):
            peer = (chip + k + 1) % GROUPS
            along_lmk(p2s.at[b, peer], p2r.at[b, k], s2.at[b], r2.at[b], peer * 2 + core).start()

    def send3(b):
        all2(b).wait_recv()
        total = p2s[b, chip].astype(F32)
        for k in range(GROUPS - 1):
            total = total + p2r[b, k].astype(F32)
        mine = BLANK + b * PIECES + core * GROUPS + chip
        fit[mine] = total.astype(BF16)
        for k in range(GROUPS - 1):
            peer = (chip + k + 1) % GROUPS
            along_lmk(fit.at[mine], fit.at[mine], s3.at[b], r3.at[b], peer * 2 + core).start()

    def send4(b):
        all3(b).wait_recv()
        copy4(b).start()

    lane = lax.broadcasted_iota(jnp.int32, (TILE, 128), 1)
    ones = jnp.where(lane < 3, 1.0, 0.0).astype(BF16)
    blank = jnp.zeros((TILE - outs, TILE), BF16)
    segs = marks // SEG

    def main(accs, kts):
        def push_points(unit, m, reg):
            at = pl.multiple_of((unit * 2 + m) * TILE, TILE)
            rows = jnp.concatenate([xm[pl.ds(at, TILE), :], ones], axis=1)
            pltpu.matmul_push_rhs(rows, reg, m, transpose=True)

        def push_tile(par, m, q, reg):
            pltpu.matmul_push_rhs(pb[par][m, pl.ds(q * TILE, TILE), :], reg, m)

        def push_fitted(unit, c, m, reg):
            pltpu.matmul_push_rhs(jnp.concatenate([fit[BLANK + unit * 2 + c], blank], axis=0), reg, m, transpose=True)

        def first_product(unit, par, m, q, reg):
            acc = accs[m]["B"]
            pltpu.matmul_acc_lhs(acc, ct[:, pl.ds(q * TILE, TILE)], reg)
            if q == 3:
                part[unit * 2 + m] = pltpu.matmul_pop(acc).astype(BF16)

        def second_product(unit, par, c, m, reg):
            tile = kts[par][lax.rem(unit // 2 + KEPT, KEPT), c, pl.ds(m * (marks // 2), marks // 2), :]
            pltpu.matmul_acc_lhs(accs[m]["C"], tile, reg)

        def unit_step(h, i, par, second):
            unit = h * HALF + i
            slot = lax.rem(unit // 2, KEPT)
            after = jnp.minimum(unit + 1, steps * UNITS - 1)
            norms = [sq[unit // UNITS, pl.ds((unit % UNITS) * 2 + m, 1), :] for m in MXUS]

            def finish(m, s):
                tile = jnp.exp(pltpu.matmul_pop(accs[m]["A"][s % RING]) + norms[m]).astype(BF16)
                rows = pl.ds(s * SEG, SEG)
                kts[par][slot, m, rows, :] = tile
                pb[par][m, rows, :] = tile

            def distances(m, low, high):
                for s in range(low, high):
                    if s >= RING:
                        finish(m, s - RING)
                    acc = accs[m]["A"][s % RING]
                    pltpu.matmul_acc_lhs(acc, ca[pl.ds(s * SEG, SEG), :], 0 if s == low else None)

            def tail():
                for s in range(segs - RING, segs):
                    for m in MXUS:
                        finish(m, s)

            def each(f, *args):
                for m in MXUS:
                    f(*(m if a is MXUS else a for a in args))

            each(distances, MXUS, 0, segs // 2 if second else 3 * segs // 8)
            if second:
                before = unit - BACK
                each(push_fitted, before, 0, MXUS, 0)
                each(first_product, unit, par, MXUS, 0, 1)
                each(push_tile, 1 - par, MXUS, 1, 1)
                each(second_product, before, 1 - par, 0, MXUS, 0)
                each(push_points, unit, MXUS, 0)
                each(first_product, unit, par, MXUS, 1, 1)
                each(push_tile, 1 - par, MXUS, 2, 1)
                each(distances, MXUS, segs // 2, segs)
                each(push_fitted, before, 1, MXUS, 0)
                each(first_product, unit, par, MXUS, 2, 1)
                each(push_tile, 1 - par, MXUS, 3, 1)
                each(second_product, before, 1 - par, 1, MXUS, 0)
                tail()
                each(push_points, after, MXUS, 0)
                each(first_product, unit, par, MXUS, 3, 1)
                each(push_tile, par, MXUS, 0, 1)
            else:
                each(push_points, unit, MXUS, 0)
                each(first_product, unit, par, MXUS, 0, 1)
                each(push_tile, 1 - par, MXUS, 1, 1)
                each(distances, MXUS, 3 * segs // 8, 3 * segs // 4)
                each(push_points, unit, MXUS, 0)
                each(first_product, unit, par, MXUS, 1, 1)
                each(push_tile, 1 - par, MXUS, 2, 1)
                each(distances, MXUS, 3 * segs // 4, segs)
                each(push_tile, 1 - par, MXUS, 3, 0)
                each(first_product, unit, par, MXUS, 2, 1)
                tail()
                each(push_tile, par, MXUS, 0, 1)
                each(first_product, unit, par, MXUS, 3, 0)
                each(push_points, after, MXUS, 0)

        for m in MXUS:
            push_points(0, m, 0)
            push_tile(1, m, 0, 1)

        def exchange(h):
            for stage, behind in ((send2, 3), (send3, 5), (send4, 7)):
                due = (h % 2 == 1) & (h >= behind)
                pl.when(due)(functools.partial(stage, (h - behind) // 2))

        end = steps - 1
        lanes = pl.ds(pl.multiple_of(chip % 2 * 128, 128), 128)
        share = GROUPS // 2

        def end1(e):
            mine = part.at[pl.ds(2 + end * PIECES + e * GROUPS + (1 - core) * share, share)]
            return along_lmk(mine, p1r.at[end, pl.ds(e * share, share)], e1.at[0, e], e1.at[1, e], other)

        def all_end(stage, e):
            return along_lmk(end_in.at[e], end_in.at[e], stage.at[0, e], stage.at[1, e], other)

        def end4(e):
            half = fit.at[pl.ds(BLANK + end * PIECES + e * GROUPS + core * share, share)]
            return along_lmk(half, half, e4.at[0, e], e4.at[1, e], other)

        def end_send2(e):
            end1(e).wait_recv()
            for g in range(share):
                own = part[2 + end * PIECES + e * GROUPS + core * share + g]
                p2s[end, e * share + g] = (own.astype(F32) + p1r[end, e * share + g].astype(F32)).astype(BF16)
            for k in range(GROUPS - 1):
                peer = (chip + k + 1) % GROUPS
                theirs = pl.ds(pl.multiple_of(peer % 2 * 128, 128), 128)
                src = p2s.at[end, e * share + peer // 2, :, theirs]
                along_lmk(src, end_in.at[e, k], e2.at[0, e], e2.at[1, e], peer * 2 + core).start()

        def end_send3(e):
            all_end(e2, e).wait_recv()
            total = p2s[end, e * share + chip // 2, :, lanes].astype(F32)
            for k in range(GROUPS - 1):
                total = total + end_in[e, k].astype(F32)
            mine = BLANK + end * PIECES + e * GROUPS + core * share + chip // 2
            fit[mine, :, lanes] = total.astype(BF16)
            for k in range(GROUPS - 1):
                peer = (chip + k + 1) % GROUPS
                piece = fit.at[mine, :, lanes]
                along_lmk(piece, piece, e3.at[0, e], e3.at[1, e], peer * 2 + core).start()

        def end_send4(e):
            all_end(e3, e).wait_recv()
            end4(e).start()

        def tiles(low, high, second):
            def half(h, carry):
                def pair(i, carry):
                    @pl.when(((i == 1) & (h < 2 * steps - 1)) | ((i == 0) & (h == 2 * steps - 1)))
                    def _():
                        pl.when((h % 2 == 0) & (h >= 2))(functools.partial(send1, h // 2 - 1))
                        exchange(h)
                        if second:
                            pl.when(h % 2 == 0)(lambda: copy4((h - LAG) // 2).wait_recv())

                    if second:
                        pl.when((i == 1) & (h == 2 * steps - 1))(lambda: end1(0).start())
                    unit_step(h, i * 2, 0, second)
                    unit_step(h, i * 2 + 1, 1, second)
                    return carry

                return lax.fori_loop(0, HALF // 2, pair, carry)

            lax.fori_loop(low, high, half, 0)

        for unit in range(LAG * HALF - BACK, 0):
            kts[unit % 2][unit // 2 + KEPT] = jnp.zeros((2, marks, TILE), BF16)
        fit[pl.ds(0, BLANK)] = jnp.zeros((BLANK, outs, TILE), BF16)
        tiles(0, LAG, False)
        tiles(LAG, 2 * steps, True)

        def second_only(first, count):
            turns = [(first + i, (count + i) % 2, c) for i in range(count) for c in range(2)]
            for unit, _, c in turns[:2]:
                for m in MXUS:
                    push_fitted(unit, c, m, c)
            for at, (unit, par, c) in enumerate(turns):
                for m in MXUS:
                    second_product(unit, par, c, m, c)
                    if at + 2 < len(turns):
                        push_fitted(turns[at + 2][0], c, m, c)

        last = steps * UNITS
        for m in MXUS:
            pltpu.matmul_acc_lhs(accs[m]["A"][0], ca[pl.ds(0, SEG), :], 0)
            push_tile(1, m, 1, 0)
            first_product(last, 0, m, 0, 1)
            push_tile(1, m, 2, 1)
            first_product(last, 0, m, 1, 0)
            push_tile(1, m, 3, 0)
            first_product(last, 0, m, 2, 1)
            first_product(last, 0, m, 3, 0)
            pltpu.matmul_pop(accs[m]["A"][0])

        end1(1).start()
        end_send2(0)
        ahead = BACK - LAG * HALF
        second_only((2 * steps - LAG) * HALF - ahead, ahead)
        end_send2(1)
        copy4(end - 3).wait_recv()
        second_only((2 * steps - LAG) * HALF, HALF)
        send3(end - 1)
        send4(end - 2)
        second_only((2 * steps - LAG + 1) * HALF, HALF)
        copy4(end - 2).wait_recv()
        second_only((2 * steps - LAG + 2) * HALF, HALF)
        end_send3(0)
        second_only((2 * steps - LAG + 3) * HALF, HALF)
        end_send3(1)
        send4(end - 1)
        copy4(end - 1).wait_recv()
        second_only((2 * steps - LAG + 4) * HALF, HALF)
        end_send4(0)
        second_only((2 * steps - LAG + 5) * HALF, HALF)
        end_send4(1)
        end4(0).wait_recv()
        second_only((2 * steps - LAG + 6) * HALF, HALF)
        end4(1).wait_recv()
        second_only((2 * steps - LAG + 7) * HALF, HALF)

        for e in range(2):
            end1(e).wait_send()
            all_end(e2, e).wait_send()
            all_end(e3, e).wait_send()
            end4(e).wait_send()
        for m in MXUS:
            total = pltpu.matmul_pop(accs[m]["C"])
            for g in range(GROUPS // 2):
                prod_t[m * (GROUPS // 2) + g] = total[g * 128 : (g + 1) * 128, :128].T[:outs]

    def acc(m):
        of = pltpu.ACC(m)
        return {"A": [of((SEG, TILE), F32)] * RING, "B": of((outs, TILE), F32), "C": of((marks // 2, TILE), F32)}

    pl.run_scoped(main, [acc(m) for m in MXUS], [pltpu.VMEM((KEPT, 2, marks, TILE), BF16)] * 2)

    for k in range(GROUPS - 1):
        peer = (here + k + 1) % GROUPS
        along_pts(prod_t.at[peer], prod_in.at[k], o_send, o_recv, peer).start()

    def sent(b, carry):
        copy1(b).wait_send()
        all2(b).wait_send()
        all3(b).wait_send()
        copy4(b).wait_send()
        return carry

    lax.fori_loop(0, steps - 1, sent, 0)
    for i in range(2):
        along_pts(rows_in, rows_in, c_send.at[i], c_recv.at[i], here).wait_send()
    along_pts(prod_in, prod_in, o_send, o_recv, here).wait_recv()
    total = prod_t[here]
    for k in range(GROUPS - 1):
        total = total + prod_in[k]
    out[...] = total
    along_pts(prod_in, prod_in, o_send, o_recv, here).wait_send()


def per_device(points, landmark_ids, coefficients):
    pts_rows, width = points.shape
    marks, outs = coefficients.shape
    steps = pts_rows // STEP
    vmem = pl.BlockSpec(memory_space=pltpu.VMEM)
    dma = pltpu.SemaphoreType.DMA
    product = pl.pallas_call(
        functools.partial(body, steps),
        out_shape=jax.ShapeDtypeStruct((outs, marks // GROUPS), F32),
        in_specs=[pl.BlockSpec(memory_space=pltpu.SMEM), vmem, pl.BlockSpec(memory_space=pl.ANY)],
        out_specs=vmem,
        scratch_shapes=[
            pltpu.VMEM((pts_rows, width), BF16),
            pltpu.VMEM((steps, PIECES, TILE), F32),
            pltpu.VMEM((marks, width + 128), BF16),
            pltpu.VMEM((marks // GROUPS, width), F32),
            pltpu.VMEM((GROUPS, marks // GROUPS, width), BF16),
            pltpu.VMEM((GROUPS - 1, marks // GROUPS, width), BF16),
            pltpu.VMEM((GROUPS, marks // GROUPS, width), BF16),
            pltpu.VMEM((2, marks, TILE), BF16),
            pltpu.VMEM((2, marks, TILE), BF16),
            pltpu.VMEM((2 + steps * PIECES, outs, TILE), BF16),
            pltpu.VMEM((steps, GROUPS, outs, TILE), BF16),
            pltpu.VMEM((steps, GROUPS, outs, TILE), BF16),
            pltpu.VMEM((steps, GROUPS - 1, outs, TILE), BF16),
            pltpu.VMEM((BLANK + steps * PIECES, outs, TILE), BF16),
            pltpu.VMEM((2, GROUPS - 1, outs, 128), BF16),
            pltpu.VMEM((GROUPS, outs, 128), F32),
            pltpu.VMEM((GROUPS - 1, outs, 128), F32),
            dma((steps,)),
            dma((2,)),
            dma((2,)),
        ]
        + [dma((steps,))] * 8
        + [dma((2, 2))] * 4
        + [dma(()), dma(())],
        compiler_params=pltpu.CompilerParams(collective_id=0, has_side_effects=True, vmem_limit_bytes=60 * 2**20),
    )(landmark_ids, coefficients.T, points)
    return product.T / (pts_rows * GROUPS)


def solution(mesh):
    placed = (P("pts", None), P("lmk"), P("lmk", None))
    with jax.sharding.use_abstract_mesh(mesh.abstract_mesh):
        return jax.shard_map(
            per_device, mesh=mesh, in_specs=placed, out_specs=P(("lmk", "pts"), None), check_vma=False
        )
```
